32 devices in a mesh: af: 8 (over y, x, core), ta: 4 (over z).
Axes of the slice: x: 2, y: 2, z: 4, core: 2. Of those that a mesh axis runs over, the one named last changes fastest.
Arguments:
- samples: bfloat16 [1024, 512, 512], P('ta', 'af'), may hold values from -6 to 6
Outputs:
- visibility: float32 [512, 128, 512], P('ta', 'af')
The draws below stay inside these ranges and needn't reach their ends.
All inputs are finite; a program needn't handle non-finite values.
Results may differ from the reference program's by a relative error of at most 0.0022.
Values may be sent and summed in bfloat16 or wider, within the bound.
No kernel may reach another device: no remote copies, remote signals or barrier semaphores. Data moves between devices by JAX's collectives and lax.ppermute only.
A program may use at most 128 MiB of HBM per device.

```python
import math
import jax
import jax.numpy as jnp

NI = 512
SAMP = 512
CH = 128
TAPS = 4
F_DEV = 256
FRAMES = 1024
N_TA = 4


def block_levels(key, shape, cuts, least, high):
    level, own = 1.0, jax.random.fold_in(key, 6)
    for axis_at, shards_of in cuts:
        draws = jnp.exp(jax.random.uniform(jax.random.fold_in(own, axis_at), (shards_of,), jnp.float32, least / len(cuts), high / len(cuts)))
        level = level * jnp.repeat(draws, shape[axis_at] // shards_of).reshape([-1 if axis == axis_at else 1 for axis in range(len(shape))])
    return level


def scatter_about(key, dims, scale, bound, pieces=(), held_as=jnp.bfloat16):
    values = jax.random.normal(key, dims, jnp.float32) * scale
    if len(pieces) > 0:
        values = block_levels(key, dims, pieces, -0.22, 0.18) * values
    return jnp.clip(values, min=-bound, max=bound).astype(held_as)


def setup_inputs(seed: int = 0) -> dict:
    streams_of = jax.random.split(jax.random.key(seed), 2)
    samples = scatter_about(streams_of[0], (FRAMES, NI, SAMP), 1.0, 6.0, ((0, 4), (1, 8)))
    return dict(samples=samples)


def tap_window(taps, samp_len):
    points = jnp.arange(taps * samp_len).astype(jnp.float32)
    centre = (taps * samp_len - 1) / 2.0
    shape_part = jnp.sinc((points - centre) / samp_len)
    taper = jnp.square(jnp.sin(math.pi * (points + 0.5) / (taps * samp_len)))
    return (shape_part * taper).reshape(taps, samp_len)

def dft_table(samp_len, channels):
    sample_idx = jnp.arange(samp_len).astype(jnp.int32)[:, None]
    chan_idx = jnp.arange(channels).astype(jnp.int32)[None, :]
    phase = (sample_idx * chan_idx % samp_len).astype(jnp.float32) * (2.0 * math.pi / samp_len)
    scale = 1.0 / math.sqrt(samp_len)
    both = jnp.stack([jnp.cos(phase) * scale, -jnp.sin(phase) * scale], axis=2)
    return both.reshape(samp_len, 2 * channels).astype(jnp.bfloat16)

def reference(samples):
    weights = tap_window(TAPS, SAMP)
    table = dft_table(SAMP, CH)
    padded = jnp.concatenate([jnp.zeros((TAPS - 1, NI, SAMP), jnp.bfloat16), samples], axis=0)
    real_sum = jnp.zeros((CH, NI, NI), jnp.float32)
    imag_sum = jnp.zeros((CH, NI, NI), jnp.float32)
    for block in range(N_TA):
        piece = padded[block * F_DEV:block * F_DEV + F_DEV + TAPS - 1]
        filtered = jnp.zeros((F_DEV, NI, SAMP), jnp.float32)
        for tap in range(TAPS):
            filtered = filtered + weights[tap][None, None, :] * piece[tap:tap + F_DEV].astype(jnp.float32)
        filtered = filtered.astype(jnp.bfloat16)
        spectrum = jnp.dot(filtered.reshape(F_DEV * NI, SAMP), table, preferred_element_type=jnp.float32)
        spectrum = spectrum.astype(jnp.bfloat16).reshape(F_DEV, NI, CH, 2).astype(jnp.float32)
        real_part = spectrum[:, :, :, 0]
        imag_part = spectrum[:, :, :, 1]
        real_sum = real_sum + jnp.einsum('fic,fjc->cij', real_part, real_part) + jnp.einsum('fic,fjc->cij', imag_part, imag_part)
        imag_sum = imag_sum + jnp.einsum('fic,fjc->cij', imag_part, real_part) - jnp.einsum('fic,fjc->cij', real_part, imag_part)
    row_idx = jnp.arange(NI)[:, None]
    col_idx = jnp.arange(NI)[None, :]
    packed = jnp.where((row_idx <= col_idx)[None], real_sum, imag_sum) / FRAMES
    return jnp.transpose(packed, (1, 0, 2))
```

```python
import functools
import math

import jax
import jax.numpy as jnp
from jax import lax
from jax.experimental import pallas as pl
from jax.experimental.pallas import tpu as pltpu
from jax.sharding import PartitionSpec as P

CH = 128
TAPS = 4
LANES = 128
ROWS = 16
VMEM = 48 * 1024 * 1024


def chunk_sizes(count):
    if count < 8:
        return [1] * count
    sizes = [1, 2]
    while sum(sizes) < count - 2:
        sizes.append(min(max(1, count // 5), count - 2 - sum(sizes)))
    return sizes + [2]


def tap_window(taps, samp_len):
    points = jnp.arange(taps * samp_len).astype(jnp.float32)
    centre = (taps * samp_len - 1) / 2.0
    shape_part = jnp.sinc((points - centre) / samp_len)
    taper = jnp.square(jnp.sin(math.pi * (points + 0.5) / (taps * samp_len)))
    return (shape_part * taper).reshape(taps, samp_len)


def dft_rows(samp_len, channels):
    sample_idx = jnp.arange(samp_len)[None, :]
    phase = (sample_idx * channels[:, None] % samp_len).astype(jnp.float32) * (
        2.0 * math.pi / samp_len
    )
    scale = 1.0 / math.sqrt(samp_len)
    both = jnp.stack([jnp.cos(phase) * scale, -jnp.sin(phase) * scale], axis=1)
    return both.reshape(-1, samp_len).astype(jnp.bfloat16)


def channelizer_body(widths, x_ref, halo_ref, w_ref, table_ref, *rest):
    outs, (carry, filt, spec) = rest[: len(widths)], rest[len(widths) :]
    block, inputs, samp_len = x_ref.shape
    tiles = block * inputs // LANES
    columns = table_ref.shape[0]

    @pl.when(pl.program_id(0) == 0)
    def _():
        carry[...] = halo_ref[...]

    def fir(group, _):
        rows = pl.ds(pl.multiple_of(group * ROWS, ROWS), ROWS)
        for lane in range(0, samp_len, LANES):
            cols = pl.ds(lane, LANES)
            weights = [
                jnp.broadcast_to(w_ref[p : p + 1, cols], (ROWS, LANES)) for p in range(TAPS)
            ]
            past = [carry[p, rows, cols].astype(jnp.float32) for p in range(TAPS - 1)]
            for f in range(block):
                past.append(x_ref[f, rows, cols].astype(jnp.float32))
                total = weights[0] * past[0]
                for p in range(1, TAPS):
                    total = total + weights[p] * past[p]
                place = pl.ds(pl.multiple_of(f * inputs + group * ROWS, ROWS), ROWS)
                filt[place, cols] = total.astype(jnp.bfloat16)
                past.pop(0)
        return 0

    lax.fori_loop(0, inputs // ROWS, fir, 0)
    carry[...] = x_ref[pl.ds(block - (TAPS - 1), TAPS - 1)]

    step = 2 if tiles % 2 == 0 else 1
    for at in range(0, tiles, step):
        product = lax.dot_general(
            table_ref[...],
            filt[pl.ds(at * LANES, step * LANES), :],
            (((1,), (1,)), ((), ())),
            preferred_element_type=jnp.float32,
        )
        for k in range(step):
            spec[pl.ds((at + k) * columns, columns), :] = product[:, k * LANES : (k + 1) * LANES]

    row = 0
    for out, width in zip(outs, widths):
        for r in range(width):
            out[r] = spec[pl.ds(row + r, tiles, stride=columns), :].astype(jnp.bfloat16)
        row += width


def channelize(samples, halo, window, table, widths):
    frames, inputs, samp_len = samples.shape
    per_tile = LANES // inputs
    block = min(frames, ROWS * per_tile)
    tiles = block // per_tile
    columns = table.shape[0]
    return pl.pallas_call(
        functools.partial(channelizer_body, widths),
        grid=(frames // block,),
        in_specs=[
            pl.BlockSpec((block, inputs, samp_len), lambda b: (b, 0, 0)),
            pl.BlockSpec(halo.shape, lambda b: (0, 0, 0)),
            pl.BlockSpec(window.shape, lambda b: (0, 0)),
            pl.BlockSpec(table.shape, lambda b: (0, 0)),
        ],
        out_specs=[pl.BlockSpec((w, tiles, LANES), lambda b: (0, b, 0)) for w in widths],
        out_shape=[
            jax.ShapeDtypeStruct((w, frames // per_tile, LANES), jnp.bfloat16) for w in widths
        ],
        scratch_shapes=[
            pltpu.VMEM((TAPS - 1, inputs, samp_len), jnp.bfloat16),
            pltpu.VMEM((block * inputs, samp_len), jnp.bfloat16),
            pltpu.VMEM((tiles * columns, LANES), jnp.float32),
        ],
        compiler_params=pltpu.CompilerParams(
            dimension_semantics=("arbitrary",), vmem_limit_bytes=VMEM
        ),
        cost_estimate=pl.CostEstimate(
            flops=2 * frames * inputs * samp_len * columns,
            bytes_accessed=frames * inputs * (samp_len + columns) * 2,
            transcendentals=0,
        ),
        name="channelizer",
    )(samples, halo, window, table)


def correlate_body(groups, inputs, scale, where_ref, *rest):
    sources, (others, own, left, turn) = rest[:groups], rest[groups:]
    per_tile = LANES // inputs
    tiles = sources[0].shape[1]
    total = groups * inputs
    me, block = where_ref[0], where_ref[1]
    half = tiles * per_tile

    for mine in range(per_tile):

        @pl.when(me % per_tile == mine)
        def _(mine=mine):
            for t in range(0, groups, per_tile):
                at = pl.multiple_of((me // per_tile ^ t // per_tile) * LANES, LANES)
                for part in range(2):
                    held = [sources[t + (mine ^ j)][part] for j in range(per_tile)]
                    for g in range(per_tile):
                        value = jnp.concatenate(
                            [h[:, g * inputs : (g + 1) * inputs] for h in held], axis=1
                        )
                        rows = pl.ds(part * half + g * tiles, tiles)
                        left[rows, pl.ds(at, LANES)] = value

    turn[pl.ds(0, half), :] = left[pl.ds(half, half), :]
    turn[pl.ds(half, half), :] = -left[pl.ds(0, half), :]

    size = own.shape[1]
    count = total // size
    row_idx = lax.broadcasted_iota(jnp.int32, (size, total), 0)
    col_idx = lax.broadcasted_iota(jnp.int32, (size, total), 1)
    dims = (((0,), (0,)), ((), ()))
    for i in range(count):
        cols = pl.ds(i * size, size)
        re = lax.dot_general(left[:, cols], left[...], dims, preferred_element_type=jnp.float32)
        im = lax.dot_general(turn[:, cols], left[...], dims, preferred_element_type=jnp.float32)
        packed = jnp.where(row_idx + i * size <= col_idx, re, im) * scale
        if count > 1:
            slot = (i - block - 1 + count) % count

            @pl.when(slot < count - 1)
            def _():
                others[jnp.minimum(slot, count - 2), 0] = packed.astype(jnp.bfloat16)

        @pl.when(block == i)
        def _():
            own[0] = packed


def correlate(where, sources, blocks, inputs, scale):
    width, tiles, _ = sources[0].shape
    chans = width // 2
    groups = len(sources)
    total = groups * inputs
    size = total // blocks
    depth = 2 * tiles * (LANES // inputs)
    return pl.pallas_call(
        functools.partial(correlate_body, groups, inputs, scale),
        grid_spec=pltpu.PrefetchScalarGridSpec(
            num_scalar_prefetch=1,
            grid=(chans,),
            in_specs=[pl.BlockSpec((2, tiles, LANES), lambda c, _: (c, 0, 0))] * groups,
            out_specs=[
                pl.BlockSpec((max(blocks - 1, 1), 1, size, total), lambda c, _: (0, c, 0, 0)),
                pl.BlockSpec((1, size, total), lambda c, _: (c, 0, 0)),
            ],
            scratch_shapes=[pltpu.VMEM((depth, total), jnp.bfloat16)] * 2,
        ),
        out_shape=[
            jax.ShapeDtypeStruct((max(blocks - 1, 1), chans, size, total), jnp.bfloat16),
            jax.ShapeDtypeStruct((chans, size, total), jnp.float32),
        ],
        compiler_params=pltpu.CompilerParams(
            dimension_semantics=("arbitrary",), vmem_limit_bytes=VMEM
        ),
        cost_estimate=pl.CostEstimate(
            flops=chans * 4 * depth * total * total,
            bytes_accessed=chans * (groups * 4 * tiles * LANES + 2 * total * total + 2 * size * total),
            transcendentals=0,
        ),
        name="correlate",
    )(where, *sources)


def line_sum(own, others, axis, block):
    count = lax.axis_size(axis)
    total = own
    held = None
    for t in range(count - 1):
        span = count - 1 - t
        right, left = (t, t + 1), (count - 1 - t, count - 2 - t)
        heading_left = block == left[0]
        if t == 0:
            sends = [others, others]
        else:
            sends = []
            for first, taken, got in ((0, 1, held[0]), (t, 0, held[1])):
                mine = lax.slice_in_dim(others, first, first + span, axis=0)
                came = lax.slice_in_dim(got, taken, taken + span, axis=0)
                sends.append((mine.astype(jnp.float32) + came.astype(jnp.float32)).astype(jnp.bfloat16))
        if count % 2 == 0:
            send = sends[0] if t == 0 else jnp.where(heading_left, sends[1], sends[0])
            got = lax.ppermute(send, axis, [right, left])
            held = [got, got]
            pick = jnp.where(block == right[1], 0, span - 1)
            total = total + lax.dynamic_index_in_dim(got, pick, 0, keepdims=False).astype(jnp.float32)
        else:
            held = [
                lax.ppermute(sends[0], axis, [right]),
                lax.ppermute(sends[1], axis, [left]),
            ]
            total = total + held[0][0].astype(jnp.float32) + held[1][span - 1].astype(jnp.float32)
    return total


def on_device(samples):
    frames, inputs, samp_len = samples.shape
    groups = lax.axis_size("af")
    blocks = lax.axis_size("ta")
    me = lax.axis_index("af")
    block = lax.axis_index("ta")
    local = CH // groups
    sizes = chunk_sizes(local)
    earlier = lax.ppermute(
        samples[frames - (TAPS - 1) :], "ta", [(i, i + 1) for i in range(blocks - 1)]
    )
    window = tap_window(TAPS, samp_len)
    order, widths, first = [], [], 0
    for size in sizes:
        for s in range(groups):
            order.append((me ^ s) * local + first + jnp.arange(size))
            widths.append(2 * size)
        first += size
    table = dft_rows(samp_len, jnp.concatenate(order))
    spectra = channelize(samples, earlier, window, table, widths)
    where = jnp.stack([me, block]).astype(jnp.int32)
    results = []
    for c in range(len(sizes)):
        mine = spectra[c * groups : (c + 1) * groups]
        turned = [mine[0]]
        for s in range(1, groups):
            turned.append(lax.ppermute(mine[s], "af", [(i, i ^ s) for i in range(groups)]))
        others, own = correlate(where, turned, blocks, inputs, 1.0 / (frames * blocks))
        results.append(line_sum(own, others, "ta", block))
    return jnp.transpose(jnp.concatenate(results, axis=0), (1, 0, 2))


def solution(mesh):
    in_specs = (P("ta", "af", None),)
    out_specs = P("ta", "af", None)
    return jax.shard_map(
        on_device, mesh=mesh, in_specs=in_specs, out_specs=out_specs, check_vma=False
    )
```

```python
import functools
import math

import jax
import jax.numpy as jnp
from jax import lax
from jax.experimental import pallas as pl
from jax.experimental.pallas import tpu as pltpu
from jax.sharding import PartitionSpec as P

CH = 128
TAPS = 4
LANES = 128
ROWS = 16
VMEM = 60 * 1024 * 1024


def chunk_sizes(count):
    if count % 16:
        return [count]
    return [4 * (count // 16), 6 * (count // 16), 6 * (count // 16)]


def in_hbm(values):
    return [pltpu.with_memory_space_constraint(v, pltpu.HBM) for v in values]


def tap_window(taps, samp_len):
    points = jnp.arange(taps * samp_len).astype(jnp.float32)
    centre = (taps * samp_len - 1) / 2.0
    shape_part = jnp.sinc((points - centre) / samp_len)
    taper = jnp.square(jnp.sin(math.pi * (points + 0.5) / (taps * samp_len)))
    return (shape_part * taper).reshape(taps, samp_len)


def dft_rows(samp_len, channels):
    sample_idx = jnp.arange(samp_len)[None, :]
    phase = (sample_idx * channels[:, None] % samp_len).astype(jnp.float32) * (
        2.0 * math.pi / samp_len
    )
    scale = 1.0 / math.sqrt(samp_len)
    both = jnp.stack([jnp.cos(phase) * scale, -jnp.sin(phase) * scale], axis=1)
    return both.reshape(-1, samp_len).astype(jnp.bfloat16)


def channelizer_body(widths, x_ref, halo_ref, w_ref, table_ref, *rest):
    outs, (carry, filt, spec) = rest[: len(widths)], rest[len(widths) :]
    block, inputs, samp_len = x_ref.shape
    tiles = block * inputs // LANES
    columns = table_ref.shape[0]

    @pl.when(pl.program_id(0) == 0)
    def _():
        carry[...] = halo_ref[...]

    def fir(group, _):
        rows = pl.ds(pl.multiple_of(group * ROWS, ROWS), ROWS)
        for lane in range(0, samp_len, LANES):
            cols = pl.ds(lane, LANES)
            weights = [
                jnp.broadcast_to(w_ref[p : p + 1, cols], (ROWS, LANES)) for p in range(TAPS)
            ]
            past = [carry[p, rows, cols].astype(jnp.float32) for p in range(TAPS - 1)]
            for f in range(block):
                past.append(x_ref[f, rows, cols].astype(jnp.float32))
                total = weights[0] * past[0]
                for p in range(1, TAPS):
                    total = total + weights[p] * past[p]
                place = pl.ds(pl.multiple_of(f * inputs + group * ROWS, ROWS), ROWS)
                filt[place, cols] = total.astype(jnp.bfloat16)
                past.pop(0)
        return 0

    lax.fori_loop(0, inputs // ROWS, fir, 0)
    carry[...] = x_ref[pl.ds(block - (TAPS - 1), TAPS - 1)]

    step = 2 if tiles % 2 == 0 else 1
    for at in range(0, tiles, step):
        product = lax.dot_general(
            table_ref[...],
            filt[pl.ds(at * LANES, step * LANES), :],
            (((1,), (1,)), ((), ())),
            preferred_element_type=jnp.float32,
        )
        for k in range(step):
            spec[pl.ds((at + k) * columns, columns), :] = product[:, k * LANES : (k + 1) * LANES]

    row = 0
    for out, (groups, width) in zip(outs, widths):
        for g in range(groups):
            for r in range(width):
                out[g, r] = spec[pl.ds(row, tiles, stride=columns), :].astype(jnp.bfloat16)
                row += 1


def channelize(samples, halo, window, table, widths):
    frames, inputs, samp_len = samples.shape
    per_tile = LANES // inputs
    block = min(frames, ROWS * per_tile)
    tiles = block // per_tile
    columns = table.shape[0]
    return pl.pallas_call(
        functools.partial(channelizer_body, widths),
        grid=(frames // block,),
        in_specs=[
            pl.BlockSpec((block, inputs, samp_len), lambda b: (b, 0, 0)),
            pl.BlockSpec(halo.shape, lambda b: (0, 0, 0)),
            pl.BlockSpec(window.shape, lambda b: (0, 0)),
            pl.BlockSpec(table.shape, lambda b: (0, 0)),
        ],
        out_specs=[pl.BlockSpec(w + (tiles, LANES), lambda b: (0, 0, b, 0)) for w in widths],
        out_shape=[
            pltpu.HBM(w + (frames // per_tile, LANES), jnp.bfloat16) for w in widths
        ],
        scratch_shapes=[
            pltpu.VMEM((TAPS - 1, inputs, samp_len), jnp.bfloat16),
            pltpu.VMEM((block * inputs, samp_len), jnp.bfloat16),
            pltpu.VMEM((tiles * columns, LANES), jnp.float32),
        ],
        compiler_params=pltpu.CompilerParams(
            dimension_semantics=("arbitrary",), vmem_limit_bytes=VMEM
        ),
        cost_estimate=pl.CostEstimate(
            flops=2 * frames * inputs * samp_len * columns,
            bytes_accessed=frames * inputs * (samp_len + columns) * 2,
            transcendentals=0,
        ),
        name="channelizer",
    )(*in_hbm([samples, halo]), window, table)


def correlate_body(inputs, scale, where_ref, source, others, own, left, turn):
    groups, _, tiles, _ = source.shape
    per_tile = LANES // inputs
    total = groups * inputs
    block = where_ref[0]
    half = tiles * per_tile

    for t in range(0, groups, per_tile):
        for part in range(2):
            for g in range(per_tile):
                rows = pl.ds(part * half + g * tiles, tiles)
                left[rows, pl.ds(t * inputs, LANES)] = jnp.concatenate(
                    [source[t + j, part, :, g * inputs : (g + 1) * inputs] for j in range(per_tile)],
                    axis=1,
                )

    turn[pl.ds(0, half), :] = left[pl.ds(half, half), :]
    turn[pl.ds(half, half), :] = -left[pl.ds(0, half), :]

    size = own.shape[1]
    dims = (((0,), (0,)), ((), ()))
    for i in range(total // size):
        cols = pl.ds(i * size, size)
        start = i * size // LANES * LANES
        stop = -(-(i + 1) * size // LANES) * LANES
        re = lax.dot_general(
            left[:, cols], left[:, start:], dims, preferred_element_type=jnp.float32
        )
        im = lax.dot_general(
            turn[:, cols], left[:, :stop], dims, preferred_element_type=jnp.float32
        )
        row_idx = lax.broadcasted_iota(jnp.int32, (size, stop - start), 0) + i * size
        col_idx = lax.broadcasted_iota(jnp.int32, (size, stop - start), 1) + start
        mixed = jnp.where(row_idx <= col_idx, re[:, : stop - start], im[:, start:])
        for value, at in ((im[:, :start], 0), (mixed, start), (re[:, stop - start :], stop)):
            if value.shape[1] == 0:
                continue
            value = value * scale
            place = pl.ds(at, value.shape[1])
            others[i, 0, :, place] = jnp.where(block == i, 0.0, value).astype(jnp.bfloat16)

            @pl.when(block == i)
            def _():
                own[0, :, place] = value


def correlate(block, source, blocks, inputs, scale):
    groups, width, tiles, _ = source.shape
    chans = width // 2
    total = groups * inputs
    size = total // blocks
    depth = 2 * tiles * (LANES // inputs)
    return pl.pallas_call(
        functools.partial(correlate_body, inputs, scale),
        grid_spec=pltpu.PrefetchScalarGridSpec(
            num_scalar_prefetch=1,
            grid=(chans,),
            in_specs=[pl.BlockSpec((groups, 2, tiles, LANES), lambda c, _: (0, c, 0, 0))],
            out_specs=[
                pl.BlockSpec((blocks, 1, size, total), lambda c, _: (0, c, 0, 0)),
                pl.BlockSpec((1, size, total), lambda c, _: (c, 0, 0)),
            ],
            scratch_shapes=[pltpu.VMEM((depth, total), jnp.bfloat16)] * 2,
        ),
        out_shape=[
            pltpu.HBM((blocks, chans, size, total), jnp.bfloat16),
            pltpu.HBM((chans, size, total), jnp.float32),
        ],
        compiler_params=pltpu.CompilerParams(
            dimension_semantics=("arbitrary",), vmem_limit_bytes=VMEM
        ),
        cost_estimate=pl.CostEstimate(
            flops=chans * 4 * depth * total * total,
            bytes_accessed=chans * (groups * 4 * tiles * LANES + 2 * total * total + 2 * size * total),
            transcendentals=0,
        ),
        name="correlate",
    )(block, *in_hbm([source]))


def settle_body(counts, *refs):
    out = refs[-1]
    k = 0
    for c, count in enumerate(counts):
        own, came = refs[2 * c], refs[2 * c + 1]
        for at in range(count):
            out[:, k, :] = own[at] + came[0, at].astype(jnp.float32)
            k += 1


def settle(owns, cames):
    counts = [own.shape[0] for own in owns]
    _, rows, total = owns[0].shape
    tall = min(rows, 32)
    specs, operands = [], []
    for own, came, count in zip(owns, cames, counts):
        operands += [own, came]
        specs.append(pl.BlockSpec((count, tall, total), lambda r: (0, r, 0)))
        specs.append(pl.BlockSpec((1, count, tall, total), lambda r: (0, 0, r, 0)))
    return pl.pallas_call(
        functools.partial(settle_body, counts),
        grid=(rows // tall,),
        in_specs=specs,
        out_specs=pl.BlockSpec((tall, sum(counts), total), lambda r: (r, 0, 0)),
        out_shape=jax.ShapeDtypeStruct((rows, sum(counts), total), jnp.float32),
        compiler_params=pltpu.CompilerParams(
            dimension_semantics=("arbitrary",), vmem_limit_bytes=VMEM
        ),
        cost_estimate=pl.CostEstimate(
            flops=rows * sum(counts) * total,
            bytes_accessed=rows * sum(counts) * total * 10,
            transcendentals=0,
        ),
        name="settle",
    )(*operands)


def on_device(samples):
    frames, inputs, samp_len = samples.shape
    groups = lax.axis_size("af")
    blocks = lax.axis_size("ta")
    local = CH // groups
    sizes = chunk_sizes(local)
    earlier = lax.ppermute(
        samples[frames - (TAPS - 1) :], "ta", [(i, i + 1) for i in range(blocks - 1)]
    )
    window = tap_window(TAPS, samp_len)
    order, widths, first = [], [], 0
    for size in sizes:
        order += [g * local + first + jnp.arange(size) for g in range(groups)]
        widths.append((groups, 2 * size))
        first += size
    table = dft_rows(samp_len, jnp.concatenate(order))
    spectra = channelize(samples, earlier, window, table, widths)
    block = lax.axis_index("ta").astype(jnp.int32)[None]
    owns, cames = [], []
    for spectrum in spectra:
        turned = lax.all_to_all(spectrum, "af", split_axis=0, concat_axis=0, tiled=True)
        others, own = correlate(block, turned, blocks, inputs, 1.0 / (frames * blocks))
        owns.append(own)
        cames.append(lax.psum_scatter(others, "ta", scatter_dimension=0, tiled=True))
    return settle(owns, cames)


def solution(mesh):
    in_specs = (P("ta", "af", None),)
    out_specs = P("ta", "af", None)
    return jax.shard_map(
        on_device, mesh=mesh, in_specs=in_specs, out_specs=out_specs, check_vma=False
    )
```

```python
import functools
import math

import jax
import jax.numpy as jnp
import numpy as np
from jax import lax
from jax.experimental import pallas as pl
from jax.experimental.pallas import tpu as pltpu
from jax.sharding import PartitionSpec as P

CH = 128
TAPS = 4
LANES = 128
ROWS = 16
PAD = 8
PER = (2, 1)
VMEM = 60 * 1024 * 1024


def chunk_plan(count, blocks):
    unit = count // 16
    swapped = 4 * unit
    if count % 16 or swapped % blocks or blocks & (blocks - 1):
        return [(count, False)]
    return [(8 * unit, False), (4 * unit, False), (swapped, True)]


def tap_window(taps, samp_len):
    points = np.arange(taps * samp_len, dtype=np.float64)
    centre = (taps * samp_len - 1) / 2.0
    shape_part = np.sinc((points - centre) / samp_len)
    taper = np.square(np.sin(math.pi * (points + 0.5) / (taps * samp_len)))
    return (shape_part * taper).reshape(taps, samp_len).astype(np.float32)


def dft_rows(samp_len, channels):
    sample_idx = np.arange(samp_len)[None, :]
    phase = (sample_idx * channels[:, None] % samp_len) * (2.0 * math.pi / samp_len)
    scale = 1.0 / math.sqrt(samp_len)
    both = np.stack([np.cos(phase) * scale, -np.sin(phase) * scale], axis=1)
    return both.reshape(-1, samp_len).astype(np.float32).astype(jnp.bfloat16)


def channelizer_body(widths, x_ref, halo_ref, w_ref, table_ref, *rest):
    outs, (carry, filt, spec) = rest[: len(widths)], rest[len(widths) :]
    block, inputs, samp_len = x_ref.shape
    tiles = block * inputs // LANES
    columns = table_ref.shape[0]
    pitch = spec.shape[0] // tiles

    @pl.when(pl.program_id(0) == 0)
    def _():
        carry[...] = halo_ref[...]

    def fir(group, _):
        rows = pl.ds(pl.multiple_of(group * ROWS, ROWS), ROWS)
        for lane in range(0, samp_len, LANES):
            cols = pl.ds(lane, LANES)
            weights = [
                jnp.broadcast_to(w_ref[p : p + 1, cols], (ROWS, LANES)) for p in range(TAPS)
            ]
            past = [carry[p, rows, cols].astype(jnp.float32) for p in range(TAPS - 1)]
            for f in range(block):
                past.append(x_ref[f, rows, cols].astype(jnp.float32))
                total = weights[0] * past[0]
                for p in range(1, TAPS):
                    total = total + weights[p] * past[p]
                place = pl.ds(pl.multiple_of(f * inputs + group * ROWS, ROWS), ROWS)
                filt[place, cols] = total.astype(jnp.bfloat16)
                past.pop(0)
        return 0

    lax.fori_loop(0, inputs // ROWS, fir, 0)
    carry[...] = x_ref[pl.ds(block - (TAPS - 1), TAPS - 1)]

    step = 2 if tiles % 2 == 0 else 1
    for at in range(0, tiles, step):
        product = lax.dot_general(
            table_ref[...],
            filt[pl.ds(at * LANES, step * LANES), :],
            (((1,), (1,)), ((), ())),
            preferred_element_type=jnp.float32,
        )
        for k in range(step):
            spec[pl.ds((at + k) * pitch, columns), :] = product[:, k * LANES : (k + 1) * LANES]

    row = 0
    for out, (groups, width) in zip(outs, widths):
        for g in range(groups):
            for r in range(width):
                out[g, r] = spec[pl.ds(row, tiles, stride=pitch), :].astype(jnp.bfloat16)
                row += 1


def channelize(samples, halo, window, table, widths):
    frames, inputs, samp_len = samples.shape
    per_tile = LANES // inputs
    block = min(frames, ROWS * per_tile)
    tiles = block // per_tile
    columns = table.shape[0]
    return pl.pallas_call(
        functools.partial(channelizer_body, widths),
        grid=(frames // block,),
        in_specs=[
            pl.BlockSpec((block, inputs, samp_len), lambda b: (b, 0, 0)),
            pl.BlockSpec(halo.shape, lambda b: (0, 0, 0)),
            pl.BlockSpec(window.shape, lambda b: (0, 0)),
            pl.BlockSpec(table.shape, lambda b: (0, 0)),
        ],
        out_specs=[pl.BlockSpec(w + (tiles, LANES), lambda b: (0, 0, b, 0)) for w in widths],
        out_shape=[
            pltpu.HBM(w + (frames // per_tile, LANES), jnp.bfloat16) for w in widths
        ],
        scratch_shapes=[
            pltpu.VMEM((TAPS - 1, inputs, samp_len), jnp.bfloat16),
            pltpu.VMEM((block * inputs, samp_len), jnp.bfloat16),
            pltpu.VMEM((tiles * (columns + PAD), LANES), jnp.float32),
        ],
        compiler_params=pltpu.CompilerParams(
            dimension_semantics=("arbitrary",), vmem_limit_bytes=VMEM
        ),
        cost_estimate=pl.CostEstimate(
            flops=2 * frames * inputs * samp_len * columns,
            bytes_accessed=frames * inputs * (samp_len + columns) * 2,
            transcendentals=0,
        ),
        name="channelizer",
    )(pltpu.with_memory_space_constraint(samples, pltpu.HBM), halo, window, table)


def correlate_body(inputs, scale, pieces, swapped, gated, tied, where_ref, source, *rest):
    rest, (left, turn) = rest[:-2], rest[-2:]
    own, sent = rest[gated + tied], rest[gated + tied + 1 : len(rest) - gated]
    groups, width, tiles, _ = source.shape
    per_tile = LANES // inputs
    total = groups * inputs
    size = own.shape[1]
    block = where_ref[0]
    half = tiles * per_tile
    depth = 2 * half
    chans = width // (2 * pieces)
    row_idx = lax.broadcasted_iota(jnp.int32, (total, total), 0)
    col_idx = lax.broadcasted_iota(jnp.int32, (total, total), 1)
    dims = (((0,), (0,)), ((), ()))
    for c in range(chans):
        for piece in range(pieces):
            base = piece * depth
            for t in range(0, groups, per_tile):
                for part in range(2):
                    at = 2 * (piece * chans + c) + part
                    for g in range(per_tile):
                        rows = pl.ds(base + part * half + g * tiles, tiles)
                        left[c, rows, pl.ds(t * inputs, LANES)] = jnp.concatenate(
                            [
                                source[t + j, at, :, g * inputs : (g + 1) * inputs]
                                for j in range(per_tile)
                            ],
                            axis=1,
                        )
            turn[c, pl.ds(base, half), :] = left[c, pl.ds(base + half, half), :]
            turn[c, pl.ds(base + half, half), :] = -left[c, pl.ds(base, half), :]
        re = lax.dot_general(left[c], left[c], dims, preferred_element_type=jnp.float32)
        im = lax.dot_general(turn[c], left[c], dims, preferred_element_type=jnp.float32)
        packed = jnp.where(row_idx <= col_idx, re, im) * scale
        for i in range(total // size):
            value = packed[i * size : (i + 1) * size]
            if swapped:
                for s in range(1, total // size):

                    @pl.when(block ^ i == s)
                    def _():
                        sent[s - 1][c] = value.astype(jnp.bfloat16)
            else:
                sent[0][i, c] = jnp.where(block == i, 0.0, value).astype(jnp.bfloat16)

            @pl.when(block == i)
            def _():
                own[c] = value


def correlate(block, source, blocks, inputs, scale, swapped, gate, tied):
    groups, width, tiles, _ = source.shape
    pieces = blocks if swapped else 1
    chans = width // (2 * pieces)
    total = groups * inputs
    size = total // blocks
    depth = 2 * tiles * (LANES // inputs) * pieces
    per = next(p for p in PER if chans % p == 0 and (p == 1 or not swapped))
    whole = pl.BlockSpec(memory_space=pltpu.HBM)
    if swapped:
        sent = [pltpu.HBM((chans, size, total), jnp.bfloat16)] * (blocks - 1)
        sent_specs = [pl.BlockSpec((chans, size, total), lambda c, _: (0, 0, 0))] * (blocks - 1)
        per = chans
    else:
        sent = [pltpu.HBM((blocks, chans, size, total), jnp.bfloat16)]
        sent_specs = [pl.BlockSpec((blocks, per, size, total), lambda c, _: (0, c, 0, 0))]
    return pl.pallas_call(
        functools.partial(correlate_body, inputs, scale, pieces, swapped, len(gate), len(tied)),
        grid_spec=pltpu.PrefetchScalarGridSpec(
            num_scalar_prefetch=1,
            grid=(chans // per,),
            in_specs=[
                pl.BlockSpec((groups, 2 * per * pieces, tiles, LANES), lambda c, _: (0, c, 0, 0))
            ]
            + [whole] * (len(gate) + len(tied)),
            out_specs=[pl.BlockSpec((per, size, total), lambda c, _: (c, 0, 0))]
            + sent_specs
            + [whole] * len(gate),
            scratch_shapes=[pltpu.VMEM((per, depth, total), jnp.bfloat16)] * 2,
        ),
        out_shape=[pltpu.HBM((chans, size, total), jnp.float32)]
        + sent
        + [pltpu.HBM(g.shape, g.dtype) for g in gate],
        input_output_aliases={2 + g: 1 + len(sent) + g for g in range(len(gate))},
        compiler_params=pltpu.CompilerParams(
            dimension_semantics=("arbitrary",), vmem_limit_bytes=VMEM
        ),
        cost_estimate=pl.CostEstimate(
            flops=chans * 4 * depth * total * total,
            bytes_accessed=chans * (groups * 4 * tiles * LANES * pieces + 2 * total * total),
            transcendentals=0,
        ),
        name="correlate",
    )(block, source, *gate, *tied)


def settle_body(parts, where_ref, *refs):
    out, k, at = refs[-1], 0, 0
    for swapped, start, stop, count in parts:
        own, came = refs[at], refs[at + 1 : at + count]
        at += count
        for c in range(start, stop):
            if swapped:
                source, c = c // own.shape[0] ^ where_ref[0], c % own.shape[0]
                value = own[c]
                for s, got in enumerate(came):
                    value = jnp.where(source == s + 1, got[c].astype(jnp.float32), value)
            else:
                value = own[c] + came[0][0, c].astype(jnp.float32)
            out[:, k, :] = value
            k += 1


def settle(block, group, parts, operands, prior, shape):
    rows, _, total = shape
    chans = sum(stop - start for _, start, stop, _ in parts)
    tall = min(rows, 32)
    specs = []
    for value in operands:
        if value.ndim == 4:
            specs.append(pl.BlockSpec((1, value.shape[1], tall, total), lambda r, _: (0, 0, r, 0)))
        else:
            specs.append(pl.BlockSpec((value.shape[0], tall, total), lambda r, _: (0, r, 0)))
    if prior is not None:
        operands = operands + [prior]
        specs.append(pl.BlockSpec(memory_space=pltpu.HBM))
    return pl.pallas_call(
        functools.partial(settle_body, parts),
        grid_spec=pltpu.PrefetchScalarGridSpec(
            num_scalar_prefetch=1,
            grid=(rows // tall,),
            in_specs=specs,
            out_specs=pl.BlockSpec((tall, chans, total), lambda r, _: (r, group, 0)),
        ),
        out_shape=jax.ShapeDtypeStruct(shape, jnp.float32),
        input_output_aliases={} if prior is None else {len(operands): 0},
        compiler_params=pltpu.CompilerParams(
            dimension_semantics=("arbitrary",), vmem_limit_bytes=VMEM
        ),
        cost_estimate=pl.CostEstimate(
            flops=rows * chans * total,
            bytes_accessed=rows * chans * total * 10,
            transcendentals=0,
        ),
        name="settle",
    )(block, *operands)


def on_device(samples):
    frames, inputs, samp_len = samples.shape
    groups = lax.axis_size("af")
    blocks = lax.axis_size("ta")
    local = CH // groups
    plan = chunk_plan(local, blocks)
    count = len(plan)
    block = lax.axis_index("ta").astype(jnp.int32)
    earlier = lax.ppermute(
        samples[frames - (TAPS - 1) :], "ta", [(i, i + 1) for i in range(blocks - 1)]
    )
    window = tap_window(TAPS, samp_len)
    firsts = [sum(size for size, _ in plan[:c]) for c in range(count)]

    def rows_of(first, size):
        return dft_rows(
            samp_len, np.concatenate([g * local + first + np.arange(size) for g in range(groups)])
        )

    tables, widths = [], []
    for first, (size, swapped) in zip(firsts, plan):
        if swapped:
            share = size // blocks
            shares = np.stack([rows_of(first + p * share, share) for p in range(blocks)])
            order = block ^ jnp.arange(blocks, dtype=jnp.int32)
            tables.append(jnp.take(shares, order, axis=0).reshape(-1, samp_len))
            widths += [(groups, 2 * share)] * blocks
        else:
            tables.append(rows_of(first, size))
            widths.append((groups, 2 * size))
    table = jnp.concatenate(tables, axis=0)
    made = list(channelize(samples, earlier, window, table, widths))
    spectra = []
    for _, swapped in plan:
        taken = blocks if swapped else 1
        spectra.append(made[:taken])
        made = made[taken:]

    def partners(values):
        return [
            lax.ppermute(value, "ta", [(i, i ^ (s + 1)) for i in range(blocks)])
            for s, value in enumerate(values)
        ]

    tied = {c: [] for c in range(count)}
    for c in range(count):
        if plan[c][1]:
            spectra[c] = spectra[c][:1] + partners(spectra[c][1:])
            tied[0] += spectra[c][1:]
    operands = []
    for c, (size, swapped) in enumerate(plan):
        ready = spectra[c][0] if not swapped else jnp.concatenate(spectra[c], axis=1)
        turned = lax.all_to_all(ready, "af", split_axis=0, concat_axis=0, tiled=True)
        gate = [spectra[c + 1][0]] if 0 < c < count - 1 else []
        own, *rest = correlate(
            block[None], turned, blocks, inputs, 1.0 / (frames * blocks), swapped, gate, tied[c]
        )
        sent = rest[: len(rest) - len(gate)]
        if gate:
            spectra[c + 1] = [rest[-1]] + spectra[c + 1][1:]
        if swapped:
            came = partners(sent)
            if c + 1 < count:
                tied[c + 1] += came
        else:
            came = [lax.psum_scatter(sent[0], "ta", scatter_dimension=0, tiled=True)]
        operands.append([own] + came)
    shape = (groups * inputs // blocks, local, groups * inputs)
    width = 8 if local % 8 == 0 else local
    result = None
    for group in range(local // width):
        parts, used = [], []
        for c, (size, swapped) in enumerate(plan):
            start = max(group * width - firsts[c], 0)
            stop = min((group + 1) * width - firsts[c], size)
            if start < stop:
                parts.append((swapped, start, stop, len(operands[c])))
                used += operands[c]
        result = settle(block[None], group, parts, used, result, shape)
    return result


def solution(mesh):
    in_specs = (P("ta", "af", None),)
    out_specs = P("ta", "af", None)
    return jax.shard_map(
        on_device, mesh=mesh, in_specs=in_specs, out_specs=out_specs, check_vma=False
    )
```

```python
import functools
import math

import jax
import jax.numpy as jnp
import numpy as np
from jax import lax
from jax.experimental import pallas as pl
from jax.experimental.pallas import tpu as pltpu
from jax.sharding import PartitionSpec as P

CH = 128
TAPS = 4
LANES = 128
ROWS = 16
PAD = 8
PER = (2, 1)
VMEM = 60 * 1024 * 1024


def chunk_plan(count, blocks):
    unit = count // 16
    swapped = 4 * unit
    if count % 16 or swapped % blocks or blocks & (blocks - 1):
        return [(count, False)]
    return [(8 * unit, False), (4 * unit, False), (swapped, True)]


def tap_window(taps, samp_len):
    points = np.arange(taps * samp_len, dtype=np.float64)
    centre = (taps * samp_len - 1) / 2.0
    shape_part = np.sinc((points - centre) / samp_len)
    taper = np.square(np.sin(math.pi * (points + 0.5) / (taps * samp_len)))
    return (shape_part * taper).reshape(taps, samp_len).astype(np.float32)


def dft_rows(samp_len, channels):
    sample_idx = np.arange(samp_len)[None, :]
    phase = (sample_idx * channels[:, None] % samp_len) * (2.0 * math.pi / samp_len)
    scale = 1.0 / math.sqrt(samp_len)
    both = np.stack([np.cos(phase) * scale, -np.sin(phase) * scale], axis=1)
    return both.reshape(-1, samp_len).astype(np.float32).astype(jnp.bfloat16)


def channelizer_body(widths, parts, where_ref, x_ref, halo_ref, w_ref, *rest):
    tables, rest = rest[:parts], rest[parts:]
    outs, (carry, table, filt, spec) = rest[: len(widths)], rest[len(widths) :]
    block, inputs, samp_len = x_ref.shape
    tiles = block * inputs // LANES
    columns = table.shape[0]
    pitch = spec.shape[0] // tiles

    @pl.when(pl.program_id(0) == 0)
    def _():
        carry[...] = halo_ref[pl.ds(halo_ref.shape[0] - (TAPS - 1), TAPS - 1)]
        row = 0
        for part in tables:
            table[pl.ds(row, part.shape[-2]), :] = part[...].reshape(part.shape[-2:])
            row += part.shape[-2]

    def fir(group, _):
        rows = pl.ds(pl.multiple_of(group * ROWS, ROWS), ROWS)
        for lane in range(0, samp_len, LANES):
            cols = pl.ds(lane, LANES)
            weights = [
                jnp.broadcast_to(w_ref[p : p + 1, cols], (ROWS, LANES)) for p in range(TAPS)
            ]
            past = [carry[p, rows, cols].astype(jnp.float32) for p in range(TAPS - 1)]
            for f in range(block):
                past.append(x_ref[f, rows, cols].astype(jnp.float32))
                total = weights[0] * past[0]
                for p in range(1, TAPS):
                    total = total + weights[p] * past[p]
                place = pl.ds(pl.multiple_of(f * inputs + group * ROWS, ROWS), ROWS)
                filt[place, cols] = total.astype(jnp.bfloat16)
                past.pop(0)
        return 0

    lax.fori_loop(0, inputs // ROWS, fir, 0)
    carry[...] = x_ref[pl.ds(block - (TAPS - 1), TAPS - 1)]

    step = 2 if tiles % 2 == 0 else 1
    for at in range(0, tiles, step):
        product = lax.dot_general(
            table[...],
            filt[pl.ds(at * LANES, step * LANES), :],
            (((1,), (1,)), ((), ())),
            preferred_element_type=jnp.float32,
        )
        for k in range(step):
            spec[pl.ds((at + k) * pitch, columns), :] = product[:, k * LANES : (k + 1) * LANES]

    row = 0
    for out, (groups, width) in zip(outs, widths):
        for g in range(groups):
            for r in range(width):
                out[g, r] = spec[pl.ds(row, tiles, stride=pitch), :].astype(jnp.bfloat16)
                row += 1


def channelize(where, samples, halo, span, window, fixed, shares, widths):
    _, inputs, samp_len = samples.shape
    per_tile = LANES // inputs
    start, stop = span
    block = frame_block(samples.shape[0], inputs)
    tiles = block // per_tile
    samples = pltpu.with_memory_space_constraint(samples, pltpu.HBM)
    if halo is None:
        halo = samples
        halo_spec = pl.BlockSpec((TAPS, inputs, samp_len), lambda b, _: (start // TAPS - 1, 0, 0))
    else:
        halo_spec = pl.BlockSpec(halo.shape, lambda b, _: (0, 0, 0))
    tables = [fixed]
    table_specs = [pl.BlockSpec(fixed.shape, lambda b, _: (0, 0))]
    columns = fixed.shape[0]
    if shares is not None:
        tables += [shares] * shares.shape[0]
        table_specs += [
            pl.BlockSpec((1,) + shares.shape[1:], lambda b, at, s=s: (at[0] ^ s, 0, 0))
            for s in range(shares.shape[0])
        ]
        columns += shares.shape[0] * shares.shape[1]
    return pl.pallas_call(
        functools.partial(channelizer_body, widths, len(tables)),
        grid_spec=pltpu.PrefetchScalarGridSpec(
            num_scalar_prefetch=1,
            grid=((stop - start) // block,),
            in_specs=[
                pl.BlockSpec((block, inputs, samp_len), lambda b, _: (b + start // block, 0, 0)),
                halo_spec,
                pl.BlockSpec(window.shape, lambda b, _: (0, 0)),
            ]
            + table_specs,
            out_specs=[pl.BlockSpec(w + (tiles, LANES), lambda b, _: (0, 0, b, 0)) for w in widths],
            scratch_shapes=[
                pltpu.VMEM((TAPS - 1, inputs, samp_len), jnp.bfloat16),
                pltpu.VMEM((columns, samp_len), jnp.bfloat16),
                pltpu.VMEM((block * inputs, samp_len), jnp.bfloat16),
                pltpu.VMEM((tiles * (columns + PAD), LANES), jnp.float32),
            ],
        ),
        out_shape=[
            pltpu.HBM(w + ((stop - start) // per_tile, LANES), jnp.bfloat16) for w in widths
        ],
        compiler_params=pltpu.CompilerParams(
            dimension_semantics=("arbitrary",), vmem_limit_bytes=VMEM
        ),
        cost_estimate=pl.CostEstimate(
            flops=2 * (stop - start) * inputs * samp_len * columns,
            bytes_accessed=(stop - start) * inputs * (samp_len + columns) * 2,
            transcendentals=0,
        ),
        name="channelizer",
    )(where, samples, halo, window, *tables)


def frame_block(frames, inputs):
    return min(frames, ROWS * (LANES // inputs))


def correlate_body(inputs, scale, count, swapped, gated, tied, where_ref, *rest):
    sources, rest = rest[:count], rest[count:]
    rest, (left, turn) = rest[:-2], rest[-2:]
    own, sent = rest[gated + tied], rest[gated + tied + 1 : len(rest) - gated]
    groups, _, width, tiles, _ = sources[0].shape
    per_tile = LANES // inputs
    total = groups * inputs
    size = own.shape[1]
    block = where_ref[0]
    half = tiles * per_tile
    row_idx = lax.broadcasted_iota(jnp.int32, (total, total), 0)
    col_idx = lax.broadcasted_iota(jnp.int32, (total, total), 1)
    dims = (((0,), (0,)), ((), ()))
    for c in range(width // 2):
        base = 0
        for source in sources:
            for piece in range(source.shape[1]):
                for t in range(0, groups, per_tile):
                    for part in range(2):
                        for g in range(per_tile):
                            rows = pl.ds(base + part * half + g * tiles, tiles)
                            left[c, rows, pl.ds(t * inputs, LANES)] = jnp.concatenate(
                                [
                                    source[
                                        t + j, piece, 2 * c + part, :, g * inputs : (g + 1) * inputs
                                    ]
                                    for j in range(per_tile)
                                ],
                                axis=1,
                            )
                turn[c, pl.ds(base, half), :] = left[c, pl.ds(base + half, half), :]
                turn[c, pl.ds(base + half, half), :] = -left[c, pl.ds(base, half), :]
                base += 2 * half
        re = lax.dot_general(left[c], left[c], dims, preferred_element_type=jnp.float32)
        im = lax.dot_general(turn[c], left[c], dims, preferred_element_type=jnp.float32)
        packed = jnp.where(row_idx <= col_idx, re, im) * scale
        for i in range(total // size):
            value = packed[i * size : (i + 1) * size]
            if swapped:
                for s in range(1, total // size):

                    @pl.when(block ^ i == s)
                    def _():
                        sent[s - 1][c] = value.astype(jnp.bfloat16)
            else:
                sent[0][i, c] = jnp.where(block == i, 0.0, value).astype(jnp.bfloat16)

            @pl.when(block == i)
            def _():
                own[c] = value


def correlate(block, sources, blocks, inputs, scale, swapped, gate, tied):
    groups, _, width, tiles, _ = sources[0].shape
    pieces = sum(source.shape[1] for source in sources)
    chans = width // 2
    total = groups * inputs
    size = total // blocks
    depth = 2 * tiles * (LANES // inputs) * pieces
    per = next(p for p in PER if chans % p == 0 and (p == 1 or not swapped))
    whole = pl.BlockSpec(memory_space=pltpu.HBM)
    if swapped:
        sent = [pltpu.HBM((chans, size, total), jnp.bfloat16)] * (blocks - 1)
        sent_specs = [pl.BlockSpec((chans, size, total), lambda c, _: (0, 0, 0))] * (blocks - 1)
        per = chans
    else:
        sent = [pltpu.HBM((blocks, chans, size, total), jnp.bfloat16)]
        sent_specs = [pl.BlockSpec((blocks, per, size, total), lambda c, _: (0, c, 0, 0))]
    return pl.pallas_call(
        functools.partial(
            correlate_body, inputs, scale, len(sources), swapped, len(gate), len(tied)
        ),
        grid_spec=pltpu.PrefetchScalarGridSpec(
            num_scalar_prefetch=1,
            grid=(chans // per,),
            in_specs=[
                pl.BlockSpec(
                    (groups, source.shape[1], 2 * per, tiles, LANES), lambda c, _: (0, 0, c, 0, 0)
                )
                for source in sources
            ]
            + [whole] * (len(gate) + len(tied)),
            out_specs=[pl.BlockSpec((per, size, total), lambda c, _: (c, 0, 0))]
            + sent_specs
            + [whole] * len(gate),
            scratch_shapes=[pltpu.VMEM((per, depth, total), jnp.bfloat16)] * 2,
        ),
        out_shape=[pltpu.HBM((chans, size, total), jnp.float32)]
        + sent
        + [pltpu.HBM(g.shape, g.dtype) for g in gate],
        input_output_aliases={
            1 + len(sources) + g: 1 + len(sent) + g for g in range(len(gate))
        },
        compiler_params=pltpu.CompilerParams(
            dimension_semantics=("arbitrary",), vmem_limit_bytes=VMEM
        ),
        cost_estimate=pl.CostEstimate(
            flops=chans * 4 * depth * total * total,
            bytes_accessed=chans * (groups * 4 * tiles * LANES * pieces + 2 * total * total),
            transcendentals=0,
        ),
        name="correlate",
    )(block, *sources, *gate, *tied)


def hold_body(*refs):
    del refs


def hold(value, tied):
    whole = pl.BlockSpec(memory_space=pltpu.HBM)
    return pl.pallas_call(
        hold_body,
        in_specs=[whole] * (1 + len(tied)),
        out_specs=whole,
        out_shape=pltpu.HBM(value.shape, value.dtype),
        input_output_aliases={0: 0},
        cost_estimate=pl.CostEstimate(flops=0, bytes_accessed=0, transcendentals=0),
        name="hold",
    )(value, *tied)


def settle_body(parts, where_ref, *refs):
    out, k, at = refs[-1], 0, 0
    for swapped, start, stop, count in parts:
        own, came = refs[at], refs[at + 1 : at + count]
        at += count
        for c in range(start, stop):
            if swapped:
                source, c = c // own.shape[0] ^ where_ref[0], c % own.shape[0]
                value = own[c]
                for s, got in enumerate(came):
                    value = jnp.where(source == s + 1, got[c].astype(jnp.float32), value)
            else:
                value = own[c] + came[0][0, c].astype(jnp.float32)
            out[:, k, :] = value
            k += 1


def settle(block, group, parts, operands, prior, shape):
    rows, _, total = shape
    chans = sum(stop - start for _, start, stop, _ in parts)
    tall = min(rows, 64)
    specs = []
    for value in operands:
        if value.ndim == 4:
            specs.append(pl.BlockSpec((1, value.shape[1], tall, total), lambda r, _: (0, 0, r, 0)))
        else:
            specs.append(pl.BlockSpec((value.shape[0], tall, total), lambda r, _: (0, r, 0)))
    if prior is not None:
        operands = operands + [prior]
        specs.append(pl.BlockSpec(memory_space=pltpu.HBM))
    return pl.pallas_call(
        functools.partial(settle_body, parts),
        grid_spec=pltpu.PrefetchScalarGridSpec(
            num_scalar_prefetch=1,
            grid=(rows // tall,),
            in_specs=specs,
            out_specs=pl.BlockSpec((tall, chans, total), lambda r, _: (r, group, 0)),
        ),
        out_shape=jax.ShapeDtypeStruct(shape, jnp.float32),
        input_output_aliases={} if prior is None else {len(operands): 0},
        compiler_params=pltpu.CompilerParams(
            dimension_semantics=("arbitrary",), vmem_limit_bytes=VMEM
        ),
        cost_estimate=pl.CostEstimate(
            flops=rows * chans * total,
            bytes_accessed=rows * chans * total * 10,
            transcendentals=0,
        ),
        name="settle",
    )(block, *operands)


def on_device(samples):
    frames, inputs, samp_len = samples.shape
    groups = lax.axis_size("af")
    blocks = lax.axis_size("ta")
    local = CH // groups
    plan = chunk_plan(local, blocks)
    count = len(plan)
    block = lax.axis_index("ta").astype(jnp.int32)
    earlier = lax.ppermute(
        samples[frames - (TAPS - 1) :], "ta", [(i, i + 1) for i in range(blocks - 1)]
    )
    window = tap_window(TAPS, samp_len)
    firsts = [sum(size for size, _ in plan[:c]) for c in range(count)]

    def rows_of(first, size):
        return dft_rows(
            samp_len, np.concatenate([g * local + first + np.arange(size) for g in range(groups)])
        )

    fixed, shares, widths = [], None, []
    for first, (size, swapped) in zip(firsts, plan):
        if swapped:
            share = size // blocks
            shares = np.stack([rows_of(first + p * share, share) for p in range(blocks)])
            widths += [(groups, 2 * share)] * blocks
        else:
            fixed.append(rows_of(first, size))
            widths.append((groups, 2 * size))
    fixed = np.concatenate(fixed)

    middle = frames // 2 if frames // frame_block(frames, inputs) % 2 == 0 else 0
    spans = [(middle, frames)] + ([(0, middle)] if middle else [])
    halves = []
    for span in spans:
        halo = earlier if span[0] == 0 else None
        halves.append(
            list(channelize(block[None], samples, halo, span, window, fixed, shares, widths))
        )

    def partners(values):
        return [
            lax.ppermute(value, "ta", [(i, i ^ (s + 1)) for i in range(blocks)])
            for s, value in enumerate(values)
        ]

    spectra = [[] for _ in plan]
    tied = {c: [] for c in range(count)}
    moved = []
    for half in halves:
        at, moving = 0, []
        for c, (_, swapped) in enumerate(plan):
            if swapped:
                moving += partners(half[at + 1 : at + blocks])
                spectra[c] += [half[at]] + moving[1 - blocks :]
                at += blocks
            else:
                spectra[c].append(hold(half[at], moved) if moved and c == 0 else half[at])
                at += 1
        moved = moving
        tied[0] += moving

    def turn(value):
        return lax.all_to_all(value, "af", split_axis=0, concat_axis=0, tiled=True)

    operands = []
    for c, (size, swapped) in enumerate(plan):
        if c == 0:
            turned = [turn(piece)[:, None] for piece in spectra[c]]
        else:
            turned = [turn(jnp.stack(spectra[c], axis=1))]
        gate = [spectra[c + 1][0]] if 0 < c < count - 1 else []
        own, *rest = correlate(
            block[None], turned, blocks, inputs, 1.0 / (frames * blocks), swapped, gate, tied[c]
        )
        sent = rest[: len(rest) - len(gate)]
        if gate:
            spectra[c + 1] = [rest[-1]] + spectra[c + 1][1:]
        if swapped:
            came = partners(sent)
            if c + 1 < count:
                tied[c + 1] += came
        else:
            came = [lax.psum_scatter(sent[0], "ta", scatter_dimension=0, tiled=True)]
        operands.append([own] + came)
    shape = (groups * inputs // blocks, local, groups * inputs)
    width = 8 if local % 8 == 0 else local
    result = None
    for group in range(local // width):
        parts, used = [], []
        for c, (size, swapped) in enumerate(plan):
            start = max(group * width - firsts[c], 0)
            stop = min((group + 1) * width - firsts[c], size)
            if start < stop:
                parts.append((swapped, start, stop, len(operands[c])))
                used += operands[c]
        result = settle(block[None], group, parts, used, result, shape)
    return result


def solution(mesh):
    in_specs = (P("ta", "af", None),)
    out_specs = P("ta", "af", None)
    return jax.shard_map(
        on_device, mesh=mesh, in_specs=in_specs, out_specs=out_specs, check_vma=False
    )
```

```python
import functools
import math

import jax
import jax.numpy as jnp
import numpy as np
from jax import lax
from jax.experimental import pallas as pl
from jax.experimental.pallas import tpu as pltpu
from jax.sharding import PartitionSpec as P

CH = 128
TAPS = 4
LANES = 128
ROWS = 16
PAD = 8
PER = (2, 1)
VMEM = 60 * 1024 * 1024


def chunk_plan(count, blocks):
    unit = count // 16
    swapped = 4 * unit
    if count % 16 or swapped % blocks or blocks & (blocks - 1):
        return [(count, False)]
    return [(8 * unit, False), (4 * unit, False), (swapped, True)]


def tap_window(taps, samp_len):
    points = np.arange(taps * samp_len, dtype=np.float64)
    centre = (taps * samp_len - 1) / 2.0
    shape_part = np.sinc((points - centre) / samp_len)
    taper = np.square(np.sin(math.pi * (points + 0.5) / (taps * samp_len)))
    return (shape_part * taper).reshape(taps, samp_len).astype(np.float32)


def dft_rows(samp_len, channels):
    sample_idx = np.arange(samp_len)[None, :]
    phase = (sample_idx * channels[:, None] % samp_len) * (2.0 * math.pi / samp_len)
    scale = 1.0 / math.sqrt(samp_len)
    both = np.stack([np.cos(phase) * scale, -np.sin(phase) * scale], axis=1)
    return both.reshape(-1, samp_len).astype(np.float32).astype(jnp.bfloat16)


def channelizer_body(widths, parts, where_ref, x_ref, halo_ref, w_ref, *rest):
    tables, rest = rest[:parts], rest[parts:]
    outs, (carry, table, filt, spec) = rest[: len(widths)], rest[len(widths) :]
    block, inputs, samp_len = x_ref.shape
    tiles = block * inputs // LANES
    columns = table.shape[0]
    pitch = spec.shape[0] // tiles

    @pl.when(pl.program_id(0) == 0)
    def _():
        carry[...] = halo_ref[pl.ds(halo_ref.shape[0] - (TAPS - 1), TAPS - 1)]
        row = 0
        for part in tables:
            table[pl.ds(row, part.shape[-2]), :] = part[...].reshape(part.shape[-2:])
            row += part.shape[-2]

    def fir(group, _):
        rows = pl.ds(pl.multiple_of(group * ROWS, ROWS), ROWS)
        for lane in range(0, samp_len, LANES):
            cols = pl.ds(lane, LANES)
            weights = [
                jnp.broadcast_to(w_ref[p : p + 1, cols], (ROWS, LANES)) for p in range(TAPS)
            ]
            past = [carry[p, rows, cols].astype(jnp.float32) for p in range(TAPS - 1)]
            for f in range(block):
                past.append(x_ref[f, rows, cols].astype(jnp.float32))
                total = weights[0] * past[0]
                for p in range(1, TAPS):
                    total = total + weights[p] * past[p]
                place = pl.ds(pl.multiple_of(f * inputs + group * ROWS, ROWS), ROWS)
                filt[place, cols] = total.astype(jnp.bfloat16)
                past.pop(0)
        return 0

    lax.fori_loop(0, inputs // ROWS, fir, 0)
    carry[...] = x_ref[pl.ds(block - (TAPS - 1), TAPS - 1)]

    step = 2 if tiles % 2 == 0 else 1
    for at in range(0, tiles, step):
        product = lax.dot_general(
            table[...],
            filt[pl.ds(at * LANES, step * LANES), :],
            (((1,), (1,)), ((), ())),
            preferred_element_type=jnp.float32,
        )
        for k in range(step):
            spec[pl.ds((at + k) * pitch, columns), :] = product[:, k * LANES : (k + 1) * LANES]

    row = 0
    for out, (groups, width) in zip(outs, widths):
        for g in range(groups):
            for r in range(width):
                out[g, r] = spec[pl.ds(row, tiles, stride=pitch), :].astype(jnp.bfloat16)
                row += 1


def channelize(where, samples, halo, span, window, fixed, shares, widths):
    _, inputs, samp_len = samples.shape
    per_tile = LANES // inputs
    start, stop = span
    block = frame_block(samples.shape[0], inputs)
    tiles = block // per_tile
    samples = pltpu.with_memory_space_constraint(samples, pltpu.HBM)
    if halo is None:
        halo = samples
        halo_spec = pl.BlockSpec((TAPS, inputs, samp_len), lambda b, _: (start // TAPS - 1, 0, 0))
    else:
        halo_spec = pl.BlockSpec(halo.shape, lambda b, _: (0, 0, 0))
    tables = [fixed]
    table_specs = [pl.BlockSpec(fixed.shape, lambda b, _: (0, 0))]
    columns = fixed.shape[0]
    if shares is not None:
        tables += [shares] * shares.shape[0]
        table_specs += [
            pl.BlockSpec((1,) + shares.shape[1:], lambda b, at, s=s: (at[0] ^ s, 0, 0))
            for s in range(shares.shape[0])
        ]
        columns += shares.shape[0] * shares.shape[1]
    return pl.pallas_call(
        functools.partial(channelizer_body, widths, len(tables)),
        grid_spec=pltpu.PrefetchScalarGridSpec(
            num_scalar_prefetch=1,
            grid=((stop - start) // block,),
            in_specs=[
                pl.BlockSpec((block, inputs, samp_len), lambda b, _: (b + start // block, 0, 0)),
                halo_spec,
                pl.BlockSpec(window.shape, lambda b, _: (0, 0)),
            ]
            + table_specs,
            out_specs=[pl.BlockSpec(w + (tiles, LANES), lambda b, _: (0, 0, b, 0)) for w in widths],
            scratch_shapes=[
                pltpu.VMEM((TAPS - 1, inputs, samp_len), jnp.bfloat16),
                pltpu.VMEM((columns, samp_len), jnp.bfloat16),
                pltpu.VMEM((block * inputs, samp_len), jnp.bfloat16),
                pltpu.VMEM((tiles * (columns + PAD), LANES), jnp.float32),
            ],
        ),
        out_shape=[
            pltpu.HBM(w + ((stop - start) // per_tile, LANES), jnp.bfloat16) for w in widths
        ],
        compiler_params=pltpu.CompilerParams(
            dimension_semantics=("arbitrary",), vmem_limit_bytes=VMEM
        ),
        cost_estimate=pl.CostEstimate(
            flops=2 * (stop - start) * inputs * samp_len * columns,
            bytes_accessed=(stop - start) * inputs * (samp_len + columns) * 2,
            transcendentals=0,
        ),
        name="channelizer",
    )(where, samples, halo, window, *tables)


def frame_block(frames, inputs):
    return min(frames, ROWS * (LANES // inputs))


def correlate_body(inputs, scale, count, swapped, gated, tied, where_ref, *rest):
    sources, rest = rest[:count], rest[count:]
    rest, (left, turn) = rest[:-2], rest[-2:]
    own, sent = rest[gated + tied], rest[gated + tied + 1 : len(rest) - gated]
    groups, _, width, tiles, _ = sources[0].shape
    per_tile = LANES // inputs
    total = groups * inputs
    size = own.shape[1]
    block = where_ref[0]
    half = tiles * per_tile
    row_idx = lax.broadcasted_iota(jnp.int32, (total, total), 0)
    col_idx = lax.broadcasted_iota(jnp.int32, (total, total), 1)
    dims = (((0,), (0,)), ((), ()))
    for c in range(width // 2):
        base = 0
        for source in sources:
            for piece in range(source.shape[1]):
                for t in range(0, groups, per_tile):
                    for part in range(2):
                        for g in range(per_tile):
                            rows = pl.ds(base + part * half + g * tiles, tiles)
                            left[c, rows, pl.ds(t * inputs, LANES)] = jnp.concatenate(
                                [
                                    source[
                                        t + j, piece, 2 * c + part, :, g * inputs : (g + 1) * inputs
                                    ]
                                    for j in range(per_tile)
                                ],
                                axis=1,
                            )
                turn[c, pl.ds(base, half), :] = left[c, pl.ds(base + half, half), :]
                turn[c, pl.ds(base + half, half), :] = -left[c, pl.ds(base, half), :]
                base += 2 * half
        re = lax.dot_general(left[c], left[c], dims, preferred_element_type=jnp.float32)
        im = lax.dot_general(turn[c], left[c], dims, preferred_element_type=jnp.float32)
        packed = jnp.where(row_idx <= col_idx, re, im) * scale
        for i in range(total // size):
            value = packed[i * size : (i + 1) * size]
            if swapped:
                for s in range(1, total // size):

                    @pl.when(block ^ i == s)
                    def _():
                        sent[s - 1][c] = value.astype(jnp.bfloat16)
            else:
                sent[0][i, c] = jnp.where(block == i, 0.0, value).astype(jnp.bfloat16)

            @pl.when(block == i)
            def _():
                own[c] = value


def correlate(block, sources, blocks, inputs, scale, swapped, gate, tied):
    groups, _, width, tiles, _ = sources[0].shape
    pieces = sum(source.shape[1] for source in sources)
    chans = width // 2
    total = groups * inputs
    size = total // blocks
    depth = 2 * tiles * (LANES // inputs) * pieces
    per = next(p for p in PER if chans % p == 0 and (p == 1 or not swapped))
    whole = pl.BlockSpec(memory_space=pltpu.HBM)
    if swapped:
        sent = [pltpu.HBM((chans, size, total), jnp.bfloat16)] * (blocks - 1)
        sent_specs = [pl.BlockSpec((chans, size, total), lambda c, _: (0, 0, 0))] * (blocks - 1)
        per = chans
    else:
        sent = [pltpu.HBM((blocks, chans, size, total), jnp.bfloat16)]
        sent_specs = [pl.BlockSpec((blocks, per, size, total), lambda c, _: (0, c, 0, 0))]
    return pl.pallas_call(
        functools.partial(
            correlate_body, inputs, scale, len(sources), swapped, len(gate), len(tied)
        ),
        grid_spec=pltpu.PrefetchScalarGridSpec(
            num_scalar_prefetch=1,
            grid=(chans // per,),
            in_specs=[
                pl.BlockSpec(
                    (groups, source.shape[1], 2 * per, tiles, LANES), lambda c, _: (0, 0, c, 0, 0)
                )
                for source in sources
            ]
            + [whole] * (len(gate) + len(tied)),
            out_specs=[pl.BlockSpec((per, size, total), lambda c, _: (c, 0, 0))]
            + sent_specs
            + [whole] * len(gate),
            scratch_shapes=[pltpu.VMEM((per, depth, total), jnp.bfloat16)] * 2,
        ),
        out_shape=[pltpu.HBM((chans, size, total), jnp.float32)]
        + sent
        + [pltpu.HBM(g.shape, g.dtype) for g in gate],
        input_output_aliases={
            1 + len(sources) + g: 1 + len(sent) + g for g in range(len(gate))
        },
        compiler_params=pltpu.CompilerParams(
            dimension_semantics=("arbitrary",), vmem_limit_bytes=VMEM
        ),
        cost_estimate=pl.CostEstimate(
            flops=chans * 4 * depth * total * total,
            bytes_accessed=chans * (groups * 4 * tiles * LANES * pieces + 2 * total * total),
            transcendentals=0,
        ),
        name="correlate",
    )(block, *sources, *gate, *tied)


def hold_body(*refs):
    del refs


def hold(value, tied):
    whole = pl.BlockSpec(memory_space=pltpu.HBM)
    return pl.pallas_call(
        hold_body,
        in_specs=[whole] * (1 + len(tied)),
        out_specs=whole,
        out_shape=pltpu.HBM(value.shape, value.dtype),
        input_output_aliases={0: 0},
        cost_estimate=pl.CostEstimate(flops=0, bytes_accessed=0, transcendentals=0),
        name="hold",
    )(value, *tied)


def settle_body(parts, where_ref, *refs):
    out, k, at = refs[-1], 0, 0
    for swapped, start, stop, count in parts:
        own, came = refs[at], refs[at + 1 : at + count]
        at += count
        for c in range(start, stop):
            if swapped:
                source, c = c // own.shape[0] ^ where_ref[0], c % own.shape[0]
                value = own[c]
                for s, got in enumerate(came):
                    value = jnp.where(source == s + 1, got[c].astype(jnp.float32), value)
            else:
                value = own[c] + came[0][0, c].astype(jnp.float32)
            out[:, k, :] = value
            k += 1


def settle(block, group, parts, operands, prior, shape):
    rows, _, total = shape
    chans = sum(stop - start for _, start, stop, _ in parts)
    tall = min(rows, 64)
    specs = []
    for value in operands:
        if value.ndim == 4:
            specs.append(pl.BlockSpec((1, value.shape[1], tall, total), lambda r, _: (0, 0, r, 0)))
        else:
            specs.append(pl.BlockSpec((value.shape[0], tall, total), lambda r, _: (0, r, 0)))
    if prior is not None:
        operands = operands + [prior]
        specs.append(pl.BlockSpec(memory_space=pltpu.HBM))
    return pl.pallas_call(
        functools.partial(settle_body, parts),
        grid_spec=pltpu.PrefetchScalarGridSpec(
            num_scalar_prefetch=1,
            grid=(rows // tall,),
            in_specs=specs,
            out_specs=pl.BlockSpec((tall, chans, total), lambda r, _: (r, group, 0)),
        ),
        out_shape=jax.ShapeDtypeStruct(shape, jnp.float32),
        input_output_aliases={} if prior is None else {len(operands): 0},
        compiler_params=pltpu.CompilerParams(
            dimension_semantics=("arbitrary",), vmem_limit_bytes=VMEM
        ),
        cost_estimate=pl.CostEstimate(
            flops=rows * chans * total,
            bytes_accessed=rows * chans * total * 10,
            transcendentals=0,
        ),
        name="settle",
    )(block, *operands)


def on_device(samples):
    frames, inputs, samp_len = samples.shape
    groups = lax.axis_size("af")
    blocks = lax.axis_size("ta")
    local = CH // groups
    plan = chunk_plan(local, blocks)
    count = len(plan)
    block = lax.axis_index("ta").astype(jnp.int32)
    earlier = lax.ppermute(
        samples[frames - (TAPS - 1) :], "ta", [(i, i + 1) for i in range(blocks - 1)]
    )
    window = tap_window(TAPS, samp_len)
    firsts = [sum(size for size, _ in plan[:c]) for c in range(count)]

    def rows_of(first, size):
        return dft_rows(
            samp_len, np.concatenate([g * local + first + np.arange(size) for g in range(groups)])
        )

    fixed, shares, widths = [], None, []
    for first, (size, swapped) in zip(firsts, plan):
        if swapped:
            share = size // blocks
            shares = np.stack([rows_of(first + p * share, share) for p in range(blocks)])
            widths += [(groups, 2 * share)] * blocks
        else:
            fixed.append(rows_of(first, size))
            widths.append((groups, 2 * size))
    fixed = np.concatenate(fixed)

    middle = frames // 2 if frames // frame_block(frames, inputs) % 2 == 0 else 0
    spans = [(middle, frames)] + ([(0, middle)] if middle else [])
    halves = []
    for span in spans:
        halo = earlier if span[0] == 0 else None
        halves.append(
            list(channelize(block[None], samples, halo, span, window, fixed, shares, widths))
        )

    def partners(values):
        return [
            lax.ppermute(value, "ta", [(i, i ^ (s + 1)) for i in range(blocks)])
            for s, value in enumerate(values)
        ]

    spectra = [[] for _ in plan]
    tied = {c: [] for c in range(count)}
    moved = []
    for half in halves:
        at, moving = 0, []
        for c, (_, swapped) in enumerate(plan):
            if swapped:
                moving += partners(half[at + 1 : at + blocks])
                spectra[c] += [half[at]] + moving[1 - blocks :]
                at += blocks
            else:
                spectra[c].append(hold(half[at], moved[:2]) if moved and c == 0 else half[at])
                at += 1
        moved = moved[2:] + moving

    def turn(value):
        return lax.all_to_all(value, "af", split_axis=0, concat_axis=0, tiled=True)

    operands = []
    for c, (size, swapped) in enumerate(plan):
        if c == 0:
            turned = [turn(piece)[:, None] for piece in spectra[c]]
        else:
            turned = [turn(jnp.stack(spectra[c], axis=1))]
        gate = [spectra[c + 1][0]] if 0 < c < count - 1 else []
        own, *rest = correlate(
            block[None], turned, blocks, inputs, 1.0 / (frames * blocks), swapped, gate, tied[c]
        )
        sent = rest[: len(rest) - len(gate)]
        if gate:
            spectra[c + 1] = [rest[-1]] + spectra[c + 1][1:]
        if swapped:
            came = partners(sent)
            if c + 1 < count:
                tied[c + 1] += came
        else:
            if c == 0 and moved:
                sent[0] = hold(sent[0], moved)
            came = [lax.psum_scatter(sent[0], "ta", scatter_dimension=0, tiled=True)]
        operands.append([own] + came)
    shape = (groups * inputs // blocks, local, groups * inputs)
    width = 8 if local % 8 == 0 else local
    result = None
    for group in range(local // width):
        parts, used = [], []
        for c, (size, swapped) in enumerate(plan):
            start = max(group * width - firsts[c], 0)
            stop = min((group + 1) * width - firsts[c], size)
            if start < stop:
                parts.append((swapped, start, stop, len(operands[c])))
                used += operands[c]
        result = settle(block[None], group, parts, used, result, shape)
    return result


def solution(mesh):
    in_specs = (P("ta", "af", None),)
    out_specs = P("ta", "af", None)
    return jax.shard_map(
        on_device, mesh=mesh, in_specs=in_specs, out_specs=out_specs, check_vma=False
    )
```

```python
import functools
import math

import jax
import jax.numpy as jnp
import numpy as np
from jax import lax
from jax.experimental import pallas as pl
from jax.experimental.pallas import tpu as pltpu
from jax.sharding import PartitionSpec as P

CH = 128
TAPS = 4
LANES = 128
ROWS = 16
PAD = 8
PER = (2, 1)
VMEM = 60 * 1024 * 1024


def chunk_plan(count, blocks):
    unit = count // 16
    swapped = 4 * unit
    if count % 16 or swapped % blocks or blocks & (blocks - 1):
        return [(count, False)]
    return [(8 * unit, False), (4 * unit, False), (swapped, True)]


def tap_window(taps, samp_len):
    points = np.arange(taps * samp_len, dtype=np.float64)
    centre = (taps * samp_len - 1) / 2.0
    shape_part = np.sinc((points - centre) / samp_len)
    taper = np.square(np.sin(math.pi * (points + 0.5) / (taps * samp_len)))
    return (shape_part * taper).reshape(taps, samp_len).astype(np.float32)


def dft_rows(samp_len, channels):
    sample_idx = np.arange(samp_len)[None, :]
    phase = (sample_idx * channels[:, None] % samp_len) * (2.0 * math.pi / samp_len)
    scale = 1.0 / math.sqrt(samp_len)
    both = np.stack([np.cos(phase) * scale, -np.sin(phase) * scale], axis=1)
    return both.reshape(-1, samp_len).astype(np.float32).astype(jnp.bfloat16)


def channelizer_body(widths, parts, where_ref, x_ref, halo_ref, w_ref, *rest):
    tables, rest = rest[:parts], rest[parts:]
    outs, (carry, table, filt, spec) = rest[: len(widths)], rest[len(widths) :]
    block, inputs, samp_len = x_ref.shape
    tiles = block * inputs // LANES
    columns = table.shape[0]
    pitch = spec.shape[0] // tiles

    @pl.when(pl.program_id(0) == 0)
    def _():
        carry[...] = halo_ref[pl.ds(halo_ref.shape[0] - (TAPS - 1), TAPS - 1)]
        row = 0
        for part in tables:
            table[pl.ds(row, part.shape[-2]), :] = part[...].reshape(part.shape[-2:])
            row += part.shape[-2]

    def fir(group, _):
        rows = pl.ds(pl.multiple_of(group * ROWS, ROWS), ROWS)
        for lane in range(0, samp_len, LANES):
            cols = pl.ds(lane, LANES)
            weights = [
                jnp.broadcast_to(w_ref[p : p + 1, cols], (ROWS, LANES)) for p in range(TAPS)
            ]
            past = [carry[p, rows, cols].astype(jnp.float32) for p in range(TAPS - 1)]
            for f in range(block):
                past.append(x_ref[f, rows, cols].astype(jnp.float32))
                total = weights[0] * past[0]
                for p in range(1, TAPS):
                    total = total + weights[p] * past[p]
                place = pl.ds(pl.multiple_of(f * inputs + group * ROWS, ROWS), ROWS)
                filt[place, cols] = total.astype(jnp.bfloat16)
                past.pop(0)
        return 0

    lax.fori_loop(0, inputs // ROWS, fir, 0)
    carry[...] = x_ref[pl.ds(block - (TAPS - 1), TAPS - 1)]

    step = 2 if tiles % 2 == 0 else 1
    for at in range(0, tiles, step):
        product = lax.dot_general(
            table[...],
            filt[pl.ds(at * LANES, step * LANES), :],
            (((1,), (1,)), ((), ())),
            preferred_element_type=jnp.float32,
        )
        for k in range(step):
            spec[pl.ds((at + k) * pitch, columns), :] = product[:, k * LANES : (k + 1) * LANES]

    row = 0
    for out, (groups, width) in zip(outs, widths):
        for g in range(groups):
            for r in range(width):
                out[g, r] = spec[pl.ds(row, tiles, stride=pitch), :].astype(jnp.bfloat16)
                row += 1


def channelize(where, samples, halo, span, window, fixed, shares, widths):
    _, inputs, samp_len = samples.shape
    per_tile = LANES // inputs
    start, stop = span
    block = frame_block(samples.shape[0], inputs)
    tiles = block // per_tile
    samples = pltpu.with_memory_space_constraint(samples, pltpu.HBM)
    if halo is None:
        halo = samples
        halo_spec = pl.BlockSpec((TAPS, inputs, samp_len), lambda b, _: (start // TAPS - 1, 0, 0))
    else:
        halo_spec = pl.BlockSpec(halo.shape, lambda b, _: (0, 0, 0))
    tables = [fixed]
    table_specs = [pl.BlockSpec(fixed.shape, lambda b, _: (0, 0))]
    columns = fixed.shape[0]
    if shares is not None:
        tables += [shares] * shares.shape[0]
        table_specs += [
            pl.BlockSpec((1,) + shares.shape[1:], lambda b, at, s=s: (at[0] ^ s, 0, 0))
            for s in range(shares.shape[0])
        ]
        columns += shares.shape[0] * shares.shape[1]
    return pl.pallas_call(
        functools.partial(channelizer_body, widths, len(tables)),
        grid_spec=pltpu.PrefetchScalarGridSpec(
            num_scalar_prefetch=1,
            grid=((stop - start) // block,),
            in_specs=[
                pl.BlockSpec((block, inputs, samp_len), lambda b, _: (b + start // block, 0, 0)),
                halo_spec,
                pl.BlockSpec(window.shape, lambda b, _: (0, 0)),
            ]
            + table_specs,
            out_specs=[pl.BlockSpec(w + (tiles, LANES), lambda b, _: (0, 0, b, 0)) for w in widths],
            scratch_shapes=[
                pltpu.VMEM((TAPS - 1, inputs, samp_len), jnp.bfloat16),
                pltpu.VMEM((columns, samp_len), jnp.bfloat16),
                pltpu.VMEM((block * inputs, samp_len), jnp.bfloat16),
                pltpu.VMEM((tiles * (columns + PAD), LANES), jnp.float32),
            ],
        ),
        out_shape=[
            pltpu.HBM(w + ((stop - start) // per_tile, LANES), jnp.bfloat16) for w in widths
        ],
        compiler_params=pltpu.CompilerParams(
            dimension_semantics=("arbitrary",), vmem_limit_bytes=VMEM
        ),
        cost_estimate=pl.CostEstimate(
            flops=2 * (stop - start) * inputs * samp_len * columns,
            bytes_accessed=(stop - start) * inputs * (samp_len + columns) * 2,
            transcendentals=0,
        ),
        name="channelizer",
    )(where, samples, halo, window, *tables)


def frame_block(frames, inputs):
    return min(frames, ROWS * (LANES // inputs))


def correlate_body(inputs, scale, count, swapped, gated, tied, where_ref, *rest):
    sources, rest = rest[:count], rest[count:]
    rest, (left, turn) = rest[:-2], rest[-2:]
    own, sent = rest[gated + tied], rest[gated + tied + 1 : len(rest) - gated]
    groups, _, width, tiles, _ = sources[0].shape
    per_tile = LANES // inputs
    total = groups * inputs
    size = own.shape[1]
    block = where_ref[0]
    half = tiles * per_tile
    row_idx = lax.broadcasted_iota(jnp.int32, (total, total), 0)
    col_idx = lax.broadcasted_iota(jnp.int32, (total, total), 1)
    dims = (((0,), (0,)), ((), ()))
    for c in range(width // 2):
        base = 0
        for source in sources:
            for piece in range(source.shape[1]):
                for t in range(0, groups, per_tile):
                    for part in range(2):
                        for g in range(per_tile):
                            rows = pl.ds(base + part * half + g * tiles, tiles)
                            left[c, rows, pl.ds(t * inputs, LANES)] = jnp.concatenate(
                                [
                                    source[
                                        t + j, piece, 2 * c + part, :, g * inputs : (g + 1) * inputs
                                    ]
                                    for j in range(per_tile)
                                ],
                                axis=1,
                            )
                turn[c, pl.ds(base, half), :] = left[c, pl.ds(base + half, half), :]
                turn[c, pl.ds(base + half, half), :] = -left[c, pl.ds(base, half), :]
                base += 2 * half
        re = lax.dot_general(left[c], left[c], dims, preferred_element_type=jnp.float32)
        im = lax.dot_general(turn[c], left[c], dims, preferred_element_type=jnp.float32)
        packed = jnp.where(row_idx <= col_idx, re, im) * scale
        for i in range(total // size):
            value = packed[i * size : (i + 1) * size]
            if swapped:
                for s in range(1, total // size):

                    @pl.when(block ^ i == s)
                    def _():
                        sent[s - 1][c] = value.astype(jnp.bfloat16)
            else:
                sent[0][i, c] = jnp.where(block == i, 0.0, value).astype(jnp.bfloat16)

            @pl.when(block == i)
            def _():
                own[c] = value


def correlate(block, sources, blocks, inputs, scale, swapped, gate, tied):
    groups, _, width, tiles, _ = sources[0].shape
    pieces = sum(source.shape[1] for source in sources)
    chans = width // 2
    total = groups * inputs
    size = total // blocks
    depth = 2 * tiles * (LANES // inputs) * pieces
    per = next(p for p in PER if chans % p == 0 and (p == 1 or not swapped))
    whole = pl.BlockSpec(memory_space=pltpu.HBM)
    if swapped:
        sent = [pltpu.HBM((chans, size, total), jnp.bfloat16)] * (blocks - 1)
        sent_specs = [pl.BlockSpec((chans, size, total), lambda c, _: (0, 0, 0))] * (blocks - 1)
        per = chans
    else:
        sent = [pltpu.HBM((blocks, chans, size, total), jnp.bfloat16)]
        sent_specs = [pl.BlockSpec((blocks, per, size, total), lambda c, _: (0, c, 0, 0))]
    return pl.pallas_call(
        functools.partial(
            correlate_body, inputs, scale, len(sources), swapped, len(gate), len(tied)
        ),
        grid_spec=pltpu.PrefetchScalarGridSpec(
            num_scalar_prefetch=1,
            grid=(chans // per,),
            in_specs=[
                pl.BlockSpec(
                    (groups, source.shape[1], 2 * per, tiles, LANES), lambda c, _: (0, 0, c, 0, 0)
                )
                for source in sources
            ]
            + [whole] * (len(gate) + len(tied)),
            out_specs=[pl.BlockSpec((per, size, total), lambda c, _: (c, 0, 0))]
            + sent_specs
            + [whole] * len(gate),
            scratch_shapes=[pltpu.VMEM((per, depth, total), jnp.bfloat16)] * 2,
        ),
        out_shape=[pltpu.HBM((chans, size, total), jnp.float32)]
        + sent
        + [pltpu.HBM(g.shape, g.dtype) for g in gate],
        input_output_aliases={
            1 + len(sources) + g: 1 + len(sent) + g for g in range(len(gate))
        },
        compiler_params=pltpu.CompilerParams(
            dimension_semantics=("arbitrary",), vmem_limit_bytes=VMEM
        ),
        cost_estimate=pl.CostEstimate(
            flops=chans * 4 * depth * total * total,
            bytes_accessed=chans * (groups * 4 * tiles * LANES * pieces + 2 * total * total),
            transcendentals=0,
        ),
        name="correlate",
    )(block, *sources, *gate, *tied)


def hold_body(*refs):
    del refs


def hold(value, tied):
    whole = pl.BlockSpec(memory_space=pltpu.HBM)
    return pl.pallas_call(
        hold_body,
        in_specs=[whole] * (1 + len(tied)),
        out_specs=whole,
        out_shape=pltpu.HBM(value.shape, value.dtype),
        input_output_aliases={0: 0},
        cost_estimate=pl.CostEstimate(flops=0, bytes_accessed=0, transcendentals=0),
        name="hold",
    )(value, *tied)


def settle_body(parts, where_ref, *refs):
    out, k, at = refs[-1], 0, 0
    for swapped, start, stop, count in parts:
        own, came = refs[at], refs[at + 1 : at + count]
        at += count
        for c in range(start, stop):
            if swapped:
                source, c = c // own.shape[0] ^ where_ref[0], c % own.shape[0]
                value = own[c]
                for s, got in enumerate(came):
                    value = jnp.where(source == s + 1, got[c].astype(jnp.float32), value)
            else:
                value = own[c] + came[0][0, c].astype(jnp.float32)
            out[:, k, :] = value
            k += 1


def settle(block, group, parts, operands, prior, shape):
    rows, _, total = shape
    chans = sum(stop - start for _, start, stop, _ in parts)
    tall = min(rows, 64)
    specs = []
    for value in operands:
        if value.ndim == 4:
            specs.append(pl.BlockSpec((1, value.shape[1], tall, total), lambda r, _: (0, 0, r, 0)))
        else:
            specs.append(pl.BlockSpec((value.shape[0], tall, total), lambda r, _: (0, r, 0)))
    if prior is not None:
        operands = operands + [prior]
        specs.append(pl.BlockSpec(memory_space=pltpu.HBM))
    return pl.pallas_call(
        functools.partial(settle_body, parts),
        grid_spec=pltpu.PrefetchScalarGridSpec(
            num_scalar_prefetch=1,
            grid=(rows // tall,),
            in_specs=specs,
            out_specs=pl.BlockSpec((tall, chans, total), lambda r, _: (r, group, 0)),
        ),
        out_shape=jax.ShapeDtypeStruct(shape, jnp.float32),
        input_output_aliases={} if prior is None else {len(operands): 0},
        compiler_params=pltpu.CompilerParams(
            dimension_semantics=("arbitrary",), vmem_limit_bytes=VMEM
        ),
        cost_estimate=pl.CostEstimate(
            flops=rows * chans * total,
            bytes_accessed=rows * chans * total * 10,
            transcendentals=0,
        ),
        name="settle",
    )(block, *operands)


def on_device(samples):
    frames, inputs, samp_len = samples.shape
    groups = lax.axis_size("af")
    blocks = lax.axis_size("ta")
    local = CH // groups
    plan = chunk_plan(local, blocks)
    count = len(plan)
    block = lax.axis_index("ta").astype(jnp.int32)
    earlier = lax.ppermute(
        samples[frames - (TAPS - 1) :], "ta", [(i, i + 1) for i in range(blocks - 1)]
    )
    window = tap_window(TAPS, samp_len)
    firsts = [sum(size for size, _ in plan[:c]) for c in range(count)]

    def rows_of(first, size):
        return dft_rows(
            samp_len, np.concatenate([g * local + first + np.arange(size) for g in range(groups)])
        )

    fixed, shares, widths = [], None, []
    for first, (size, swapped) in zip(firsts, plan):
        if swapped:
            share = size // blocks
            shares = np.stack([rows_of(first + p * share, share) for p in range(blocks)])
            widths += [(groups, 2 * share)] * blocks
        else:
            fixed.append(rows_of(first, size))
            widths.append((groups, 2 * size))
    fixed = np.concatenate(fixed)

    middle = frames // 2 if frames // frame_block(frames, inputs) % 2 == 0 else 0
    spans = [(middle, frames)] + ([(0, middle)] if middle else [])
    halves = []
    for span in spans:
        halo = earlier if span[0] == 0 else None
        halves.append(
            list(channelize(block[None], samples, halo, span, window, fixed, shares, widths))
        )

    def partners(values):
        return [
            lax.ppermute(value, "ta", [(i, i ^ (s + 1)) for i in range(blocks)])
            for s, value in enumerate(values)
        ]

    spectra = [[] for _ in plan]
    tied = {c: [] for c in range(count)}
    moved = []
    for half in halves:
        at, moving = 0, []
        for c, (_, swapped) in enumerate(plan):
            if swapped:
                moving += partners(half[at + 1 : at + blocks])
                spectra[c] += [half[at]] + moving[1 - blocks :]
                at += blocks
            else:
                spectra[c].append(hold(half[at], moved[::2]) if moved and c == 0 else half[at])
                at += 1
        moved = moved[1:2] + moving

    def turn(value):
        return lax.all_to_all(value, "af", split_axis=0, concat_axis=0, tiled=True)

    operands = []
    for c, (size, swapped) in enumerate(plan):
        if c == 0:
            turned = [turn(piece)[:, None] for piece in spectra[c]]
        else:
            turned = [turn(jnp.stack(spectra[c], axis=1))]
        gate = [spectra[c + 1][0]] if 0 < c < count - 1 else []
        own, *rest = correlate(
            block[None], turned, blocks, inputs, 1.0 / (frames * blocks), swapped, gate, tied[c]
        )
        sent = rest[: len(rest) - len(gate)]
        if gate:
            spectra[c + 1] = [rest[-1]] + spectra[c + 1][1:]
        if swapped:
            came = partners(sent)
            if c + 1 < count:
                tied[c + 1] += came
        else:
            if c == 0 and moved:
                sent[0] = hold(sent[0], moved)
            came = [lax.psum_scatter(sent[0], "ta", scatter_dimension=0, tiled=True)]
        operands.append([own] + came)
    shape = (groups * inputs // blocks, local, groups * inputs)
    width = 8 if local % 8 == 0 else local
    result = None
    for group in range(local // width):
        parts, used = [], []
        for c, (size, swapped) in enumerate(plan):
            start = max(group * width - firsts[c], 0)
            stop = min((group + 1) * width - firsts[c], size)
            if start < stop:
                parts.append((swapped, start, stop, len(operands[c])))
                used += operands[c]
        result = settle(block[None], group, parts, used, result, shape)
    return result


def solution(mesh):
    in_specs = (P("ta", "af", None),)
    out_specs = P("ta", "af", None)
    return jax.shard_map(
        on_device, mesh=mesh, in_specs=in_specs, out_specs=out_specs, check_vma=False
    )
```

```python
import functools
import math

import jax
import jax.numpy as jnp
import numpy as np
from jax import lax
from jax.experimental import pallas as pl
from jax.experimental.pallas import tpu as pltpu
from jax.sharding import PartitionSpec as P

CH = 128
TAPS = 4
LANES = 128
ROWS = 16
PAD = 4
PER = (2, 1)
VMEM = 60 * 1024 * 1024


def chunk_plan(count, blocks):
    unit = count // 16
    swapped = 4 * unit
    if count % 16 or swapped % blocks or blocks & (blocks - 1):
        return [(count, False)]
    return [(8 * unit, False), (4 * unit, False), (swapped, True)]


def tap_window(taps, samp_len):
    points = np.arange(taps * samp_len, dtype=np.float64)
    centre = (taps * samp_len - 1) / 2.0
    shape_part = np.sinc((points - centre) / samp_len)
    taper = np.square(np.sin(math.pi * (points + 0.5) / (taps * samp_len)))
    return (shape_part * taper).reshape(taps, samp_len).astype(np.float32)


def dft_rows(samp_len, channels):
    sample_idx = np.arange(samp_len)[None, :]
    phase = (sample_idx * channels[:, None] % samp_len) * (2.0 * math.pi / samp_len)
    scale = 1.0 / math.sqrt(samp_len)
    both = np.stack([np.cos(phase) * scale, -np.sin(phase) * scale], axis=1)
    return both.reshape(-1, samp_len).astype(np.float32).astype(jnp.bfloat16)


def channelizer_body(widths, parts, where_ref, x_ref, halo_ref, w_ref, *rest):
    tables, rest = rest[:parts], rest[parts:]
    outs, (carry, table, filt, spec) = rest[: len(widths)], rest[len(widths) :]
    block, inputs, samp_len = x_ref.shape
    tiles = block * inputs // LANES
    columns = table.shape[0]
    pitch = spec.shape[0] // tiles

    @pl.when(pl.program_id(0) == 0)
    def _():
        carry[...] = halo_ref[pl.ds(halo_ref.shape[0] - (TAPS - 1), TAPS - 1)]
        row = 0
        for part in tables:
            table[pl.ds(row, part.shape[-2]), :] = part[...].reshape(part.shape[-2:])
            row += part.shape[-2]

    def fir(group, _):
        rows = pl.ds(pl.multiple_of(group * ROWS, ROWS), ROWS)
        for lane in range(0, samp_len, LANES):
            cols = pl.ds(lane, LANES)
            weights = [
                jnp.broadcast_to(w_ref[p : p + 1, cols], (ROWS, LANES)) for p in range(TAPS)
            ]
            past = [carry[p, rows, cols].astype(jnp.float32) for p in range(TAPS - 1)]
            for f in range(block):
                past.append(x_ref[f, rows, cols].astype(jnp.float32))
                total = weights[0] * past[0]
                for p in range(1, TAPS):
                    total = total + weights[p] * past[p]
                place = pl.ds(pl.multiple_of(f * inputs + group * ROWS, ROWS), ROWS)
                filt[place, cols] = total.astype(jnp.bfloat16)
                past.pop(0)
        return 0

    lax.fori_loop(0, inputs // ROWS, fir, 0)
    carry[...] = x_ref[pl.ds(block - (TAPS - 1), TAPS - 1)]

    step = 2 if tiles % 2 == 0 else 1
    for at in range(0, tiles, step):
        product = lax.dot_general(
            table[...],
            filt[pl.ds(at * LANES, step * LANES), :],
            (((1,), (1,)), ((), ())),
            preferred_element_type=jnp.float32,
        )
        for k in range(step):
            spec[pl.ds((at + k) * pitch, columns), :] = product[:, k * LANES : (k + 1) * LANES]

    row = 0
    for out, (groups, width) in zip(outs, widths):
        for g in range(groups):
            for r in range(width):
                out[g, r] = spec[pl.ds(row, tiles, stride=pitch), :].astype(jnp.bfloat16)
                row += 1


def channelize(where, samples, halo, span, window, fixed, shares, widths):
    _, inputs, samp_len = samples.shape
    per_tile = LANES // inputs
    start, stop = span
    block = frame_block(samples.shape[0], inputs)
    tiles = block // per_tile
    samples = pltpu.with_memory_space_constraint(samples, pltpu.HBM)
    if halo is None:
        halo = samples
        halo_spec = pl.BlockSpec((TAPS, inputs, samp_len), lambda b, _: (start // TAPS - 1, 0, 0))
    else:
        halo_spec = pl.BlockSpec(halo.shape, lambda b, _: (0, 0, 0))
    tables = [fixed]
    table_specs = [pl.BlockSpec(fixed.shape, lambda b, _: (0, 0))]
    columns = fixed.shape[0]
    if shares is not None:
        tables += [shares] * shares.shape[0]
        table_specs += [
            pl.BlockSpec((1,) + shares.shape[1:], lambda b, at, s=s: (at[0] ^ s, 0, 0))
            for s in range(shares.shape[0])
        ]
        columns += shares.shape[0] * shares.shape[1]
    return pl.pallas_call(
        functools.partial(channelizer_body, widths, len(tables)),
        grid_spec=pltpu.PrefetchScalarGridSpec(
            num_scalar_prefetch=1,
            grid=((stop - start) // block,),
            in_specs=[
                pl.BlockSpec((block, inputs, samp_len), lambda b, _: (b + start // block, 0, 0)),
                halo_spec,
                pl.BlockSpec(window.shape, lambda b, _: (0, 0)),
            ]
            + table_specs,
            out_specs=[pl.BlockSpec(w + (tiles, LANES), lambda b, _: (0, 0, b, 0)) for w in widths],
            scratch_shapes=[
                pltpu.VMEM((TAPS - 1, inputs, samp_len), jnp.bfloat16),
                pltpu.VMEM((columns, samp_len), jnp.bfloat16),
                pltpu.VMEM((block * inputs, samp_len), jnp.bfloat16),
                pltpu.VMEM((tiles * (columns + PAD), LANES), jnp.float32),
            ],
        ),
        out_shape=[
            pltpu.HBM(w + ((stop - start) // per_tile, LANES), jnp.bfloat16) for w in widths
        ],
        compiler_params=pltpu.CompilerParams(
            dimension_semantics=("arbitrary",), vmem_limit_bytes=VMEM
        ),
        cost_estimate=pl.CostEstimate(
            flops=2 * (stop - start) * inputs * samp_len * columns,
            bytes_accessed=(stop - start) * inputs * (samp_len + columns) * 2,
            transcendentals=0,
        ),
        name="channelizer",
    )(where, samples, halo, window, *tables)


def frame_block(frames, inputs):
    return min(frames, ROWS * (LANES // inputs))


def correlate_body(inputs, scale, count, swapped, gated, tied, where_ref, *rest):
    sources, rest = rest[:count], rest[count:]
    rest, (left, turn) = rest[:-2], rest[-2:]
    own, sent = rest[gated + tied], rest[gated + tied + 1 : len(rest) - gated]
    groups, _, width, tiles, _ = sources[0].shape
    per_tile = LANES // inputs
    total = groups * inputs
    size = own.shape[1]
    block = where_ref[0]
    half = tiles * per_tile
    row_idx = lax.broadcasted_iota(jnp.int32, (total, total), 0)
    col_idx = lax.broadcasted_iota(jnp.int32, (total, total), 1)
    dims = (((0,), (0,)), ((), ()))
    for c in range(width // 2):
        base = 0
        for source in sources:
            for piece in range(source.shape[1]):
                for t in range(0, groups, per_tile):
                    for part in range(2):
                        for g in range(per_tile):
                            rows = pl.ds(base + part * half + g * tiles, tiles)
                            left[c, rows, pl.ds(t * inputs, LANES)] = jnp.concatenate(
                                [
                                    source[
                                        t + j, piece, 2 * c + part, :, g * inputs : (g + 1) * inputs
                                    ]
                                    for j in range(per_tile)
                                ],
                                axis=1,
                            )
                turn[c, pl.ds(base, half), :] = left[c, pl.ds(base + half, half), :]
                turn[c, pl.ds(base + half, half), :] = -left[c, pl.ds(base, half), :]
                base += 2 * half
        re = lax.dot_general(left[c], left[c], dims, preferred_element_type=jnp.float32)
        im = lax.dot_general(turn[c], left[c], dims, preferred_element_type=jnp.float32)
        packed = jnp.where(row_idx <= col_idx, re, im) * scale
        for i in range(total // size):
            value = packed[i * size : (i + 1) * size]
            if swapped:
                for s in range(1, total // size):

                    @pl.when(block ^ i == s)
                    def _():
                        sent[s - 1][c] = value.astype(jnp.bfloat16)
            else:
                sent[0][i, c] = jnp.where(block == i, 0.0, value).astype(jnp.bfloat16)

            @pl.when(block == i)
            def _():
                own[c] = value


def correlate(block, sources, blocks, inputs, scale, swapped, gate, tied):
    groups, _, width, tiles, _ = sources[0].shape
    pieces = sum(source.shape[1] for source in sources)
    chans = width // 2
    total = groups * inputs
    size = total // blocks
    depth = 2 * tiles * (LANES // inputs) * pieces
    per = next(p for p in PER if chans % p == 0 and (p == 1 or not swapped))
    whole = pl.BlockSpec(memory_space=pltpu.HBM)
    if swapped:
        sent = [pltpu.HBM((chans, size, total), jnp.bfloat16)] * (blocks - 1)
        sent_specs = [pl.BlockSpec((chans, size, total), lambda c, _: (0, 0, 0))] * (blocks - 1)
        per = chans
    else:
        sent = [pltpu.HBM((blocks, chans, size, total), jnp.bfloat16)]
        sent_specs = [pl.BlockSpec((blocks, per, size, total), lambda c, _: (0, c, 0, 0))]
    return pl.pallas_call(
        functools.partial(
            correlate_body, inputs, scale, len(sources), swapped, len(gate), len(tied)
        ),
        grid_spec=pltpu.PrefetchScalarGridSpec(
            num_scalar_prefetch=1,
            grid=(chans // per,),
            in_specs=[
                pl.BlockSpec(
                    (groups, source.shape[1], 2 * per, tiles, LANES), lambda c, _: (0, 0, c, 0, 0)
                )
                for source in sources
            ]
            + [whole] * (len(gate) + len(tied)),
            out_specs=[pl.BlockSpec((per, size, total), lambda c, _: (c, 0, 0))]
            + sent_specs
            + [whole] * len(gate),
            scratch_shapes=[pltpu.VMEM((per, depth, total), jnp.bfloat16)] * 2,
        ),
        out_shape=[pltpu.HBM((chans, size, total), jnp.float32)]
        + sent
        + [pltpu.HBM(g.shape, g.dtype) for g in gate],
        input_output_aliases={
            1 + len(sources) + g: 1 + len(sent) + g for g in range(len(gate))
        },
        compiler_params=pltpu.CompilerParams(
            dimension_semantics=("arbitrary",), vmem_limit_bytes=VMEM
        ),
        cost_estimate=pl.CostEstimate(
            flops=chans * 4 * depth * total * total,
            bytes_accessed=chans * (groups * 4 * tiles * LANES * pieces + 2 * total * total),
            transcendentals=0,
        ),
        name="correlate",
    )(block, *sources, *gate, *tied)


def hold_body(*refs):
    del refs


def hold(value, tied):
    whole = pl.BlockSpec(memory_space=pltpu.HBM)
    return pl.pallas_call(
        hold_body,
        in_specs=[whole] * (1 + len(tied)),
        out_specs=whole,
        out_shape=pltpu.HBM(value.shape, value.dtype),
        input_output_aliases={0: 0},
        cost_estimate=pl.CostEstimate(flops=0, bytes_accessed=0, transcendentals=0),
        name="hold",
    )(value, *tied)


def settle_body(parts, where_ref, *refs):
    out, k, at = refs[-1], 0, 0
    for swapped, start, stop, count in parts:
        own, came = refs[at], refs[at + 1 : at + count]
        at += count
        for c in range(start, stop):
            if swapped:
                source, c = c // own.shape[0] ^ where_ref[0], c % own.shape[0]
                value = own[c]
                for s, got in enumerate(came):
                    value = jnp.where(source == s + 1, got[c].astype(jnp.float32), value)
            else:
                value = own[c] + came[0][0, c].astype(jnp.float32)
            out[:, k, :] = value
            k += 1


def settle(block, group, parts, operands, prior, shape):
    rows, _, total = shape
    chans = sum(stop - start for _, start, stop, _ in parts)
    tall = min(rows, 64)
    specs = []
    for value in operands:
        if value.ndim == 4:
            specs.append(pl.BlockSpec((1, value.shape[1], tall, total), lambda r, _: (0, 0, r, 0)))
        else:
            specs.append(pl.BlockSpec((value.shape[0], tall, total), lambda r, _: (0, r, 0)))
    if prior is not None:
        operands = operands + [prior]
        specs.append(pl.BlockSpec(memory_space=pltpu.HBM))
    return pl.pallas_call(
        functools.partial(settle_body, parts),
        grid_spec=pltpu.PrefetchScalarGridSpec(
            num_scalar_prefetch=1,
            grid=(rows // tall,),
            in_specs=specs,
            out_specs=pl.BlockSpec((tall, chans, total), lambda r, _: (r, group, 0)),
        ),
        out_shape=jax.ShapeDtypeStruct(shape, jnp.float32),
        input_output_aliases={} if prior is None else {len(operands): 0},
        compiler_params=pltpu.CompilerParams(
            dimension_semantics=("arbitrary",), vmem_limit_bytes=VMEM
        ),
        cost_estimate=pl.CostEstimate(
            flops=rows * chans * total,
            bytes_accessed=rows * chans * total * 10,
            transcendentals=0,
        ),
        name="settle",
    )(block, *operands)


def on_device(samples):
    frames, inputs, samp_len = samples.shape
    groups = lax.axis_size("af")
    blocks = lax.axis_size("ta")
    local = CH // groups
    plan = chunk_plan(local, blocks)
    count = len(plan)
    block = lax.axis_index("ta").astype(jnp.int32)
    earlier = lax.ppermute(
        samples[frames - (TAPS - 1) :], "ta", [(i, i + 1) for i in range(blocks - 1)]
    )
    window = tap_window(TAPS, samp_len)
    firsts = [sum(size for size, _ in plan[:c]) for c in range(count)]

    def rows_of(first, size):
        return dft_rows(
            samp_len, np.concatenate([g * local + first + np.arange(size) for g in range(groups)])
        )

    fixed, shares, widths = [], None, []
    for first, (size, swapped) in zip(firsts, plan):
        if swapped:
            share = size // blocks
            shares = np.stack([rows_of(first + p * share, share) for p in range(blocks)])
            widths += [(groups, 2 * share)] * blocks
        else:
            fixed.append(rows_of(first, size))
            widths.append((groups, 2 * size))
    fixed = np.concatenate(fixed)

    middle = frames // 2 if frames // frame_block(frames, inputs) % 2 == 0 else 0
    spans = [(middle, frames)] + ([(0, middle)] if middle else [])
    halves = []
    for span in spans:
        halo = earlier if span[0] == 0 else None
        halves.append(
            list(channelize(block[None], samples, halo, span, window, fixed, shares, widths))
        )

    def partners(values):
        return [
            lax.ppermute(value, "ta", [(i, i ^ (s + 1)) for i in range(blocks)])
            for s, value in enumerate(values)
        ]

    spectra = [[] for _ in plan]
    tied = {c: [] for c in range(count)}
    moved = []
    for half in halves:
        at, moving = 0, []
        for c, (_, swapped) in enumerate(plan):
            if swapped:
                moving += partners(half[at + 1 : at + blocks])
                spectra[c] += [half[at]] + moving[1 - blocks :]
                at += blocks
            else:
                spectra[c].append(hold(half[at], moved[::2]) if moved and c == 0 else half[at])
                at += 1
        moved = moved[1:2] + moving

    def turn(value):
        return lax.all_to_all(value, "af", split_axis=0, concat_axis=0, tiled=True)

    operands = []
    for c, (size, swapped) in enumerate(plan):
        if c == 0:
            turned = [turn(piece)[:, None] for piece in spectra[c]]
        else:
            turned = [turn(jnp.stack(spectra[c], axis=1))]
        gate = [spectra[c + 1][0]] if 0 < c < count - 1 else []
        own, *rest = correlate(
            block[None], turned, blocks, inputs, 1.0 / (frames * blocks), swapped, gate, tied[c]
        )
        sent = rest[: len(rest) - len(gate)]
        if gate:
            spectra[c + 1] = [rest[-1]] + spectra[c + 1][1:]
        if swapped:
            came = partners(sent)
            if c + 1 < count:
                tied[c + 1] += came
        else:
            if c == 0 and moved:
                sent[0] = hold(sent[0], moved)
            came = [lax.psum_scatter(sent[0], "ta", scatter_dimension=0, tiled=True)]
        operands.append([own] + came)
    shape = (groups * inputs // blocks, local, groups * inputs)
    width = 8 if local % 8 == 0 else local
    result = None
    for group in range(local // width):
        parts, used = [], []
        for c, (size, swapped) in enumerate(plan):
            start = max(group * width - firsts[c], 0)
            stop = min((group + 1) * width - firsts[c], size)
            if start < stop:
                parts.append((swapped, start, stop, len(operands[c])))
                used += operands[c]
        result = settle(block[None], group, parts, used, result, shape)
    return result


def solution(mesh):
    in_specs = (P("ta", "af", None),)
    out_specs = P("ta", "af", None)
    return jax.shard_map(
        on_device, mesh=mesh, in_specs=in_specs, out_specs=out_specs, check_vma=False
    )
```
